256 devices in a mesh: dp: 32 (over x, y, core), tensor: 8 (over z).
Axes of the slice: x: 4, y: 4, z: 8, core: 2. Of those that a mesh axis runs over, the one named last changes fastest.
Arguments:
- queries: bfloat16 [16384, 8192], P('dp', 'tensor'), may hold values from -8 to 8
- suffix_kv: bfloat16 [16384, 2048], P('dp', 'tensor'), may hold values from -8 to 8
- prefix_key_value: bfloat16 [256, 64, 2048], P('dp', None, 'tensor'), may hold values from -5 to 5
- answer_ids: int32 [32, 512], P('dp'), may hold values from 0 to 15, never falling along the last dimension, each value on 1 to 64 neighbouring positions
- read_tiles: int32 [32, 26], P('dp'), may hold values from 0 to 255, as said below
- visible: int32 [32, 2, 26], P('dp'), may hold values 0 or 1
- out_weight: bfloat16 [8192, 4096], P('tensor', 'dp'), may hold values from -0.1875 to 0.1875
Outputs:
- scored: bfloat16 [16384, 4096], P('dp', 'tensor')
The draws below stay inside these ranges and needn't reach their ends.
Inputs may be any that keep to these rules, and one draw needn't show every extreme that they name: `answer_ids`: along a row answer numbers never fall; each answer has 1 to 64 tokens, and some answer has exactly that many. `read_tiles`: tile t is stored by data group t // 8. A row lists 26 distinct tiles in no fixed order. The same 2 tiles, stored by one data group, stand in every row; of the other tiles of a row at most one is stored by any one data group.
All inputs are finite; a program needn't handle non-finite values. No bound on the sum of `visible` on one device may be relied on, other than what follows from the above.
Results may differ from the reference program's by a relative error of at most 0.0052.
Values may be sent and summed in bfloat16 or wider, within the bound.
A program may use at most 64 MiB of HBM per device.

```python
import math
import jax
import jax.numpy as jnp
import numpy as np
from jax import lax

QUERY_HEADS = 64
KEY_VALUE_HEADS = 8
HEAD_WIDTH = 128
D_OUT = 4096
T_DEV = 512
ANS_DEV = 16
QG = 2
TILE_TOKENS = 64
TILE_DEV = 8
CAP = 2
READ_TILE_COUNT = 26
ANSWER_TOKENS = 16384
TOTAL_TILE_COUNT = 256
N_DP = 32


def attention_pair(base_key):
    query_seed, paired_random_seed = jax.random.split(base_key, 2)
    query_draw = jnp.clip(2.0 * jax.random.normal(query_seed, (ANSWER_TOKENS, QUERY_HEADS * HEAD_WIDTH), jnp.float32), -8.0, 8.0)
    paired_sample = jnp.clip(jax.random.normal(paired_random_seed, (ANSWER_TOKENS, 2 * KEY_VALUE_HEADS * HEAD_WIDTH), jnp.float32), -5.0, 5.0)
    return (query_draw, paired_sample)


def draw_queries(key, part):
    return attention_pair(jax.random.fold_in(key, 11))[0].astype(jnp.bfloat16)


def draw_suffix_kv(key, part):
    return attention_pair(jax.random.fold_in(key, 11))[1].astype(jnp.bfloat16)


def draw_read_tiles(key, part):
    hot_seed, root_seed, group_seed = jax.random.split(key, 3)
    hot_owner = jax.random.randint(hot_seed, (), 0, N_DP)
    root_tiles = jax.random.permutation(root_seed, TILE_DEV)[:CAP] + hot_owner * TILE_DEV

    def one_group(group_key):
        owner_seed, local_seed, order_seed = jax.random.split(group_key, 3)
        others = jax.random.permutation(owner_seed, N_DP - 1)[:READ_TILE_COUNT - CAP]
        others = others + (others >= hot_owner).astype(others.dtype)
        local_tile = jax.random.randint(local_seed, (READ_TILE_COUNT - CAP,), 0, TILE_DEV)
        listed = jnp.concatenate([root_tiles.astype(jnp.int32), (others * TILE_DEV + local_tile).astype(jnp.int32)])
        return listed[jax.random.permutation(order_seed, READ_TILE_COUNT)]
    return jax.vmap(one_group)(jax.random.split(group_seed, N_DP)).astype(jnp.int32)


def touch_ends(entries, key, least, high):
    extent = entries.shape
    place = [jax.random.randint(jax.random.fold_in(key, axis), (), 0, extent[axis]) for axis in range(len(extent))]
    entries = entries.at[tuple(place)].set(least)
    longest = extent.index(max(extent))
    place[longest] = (place[longest] + 1) % extent[longest]
    return entries.at[tuple(place)].set(high)


def level_of(key, dims, shards, least, high):
    loudness = 1.0
    for dim, parts in shards:
        steps = jax.random.uniform(jax.random.fold_in(jax.random.fold_in(key, 6), dim), (parts,), jnp.float32, least / len(shards), high / len(shards))
        loudness = loudness * jnp.repeat(jnp.exp(steps), dims[dim] // parts).reshape((-1,) + (1,) * (len(dims) - 1 - dim))
    return loudness


def length_profile(count, total, limit, slope):
    weights = [(1 << 20) // math.isqrt(grade ** slope) + 1 for grade in range(2, count + 1)]
    spare, holding = total - limit - (count - 1), [1] * (count - 1)
    while spare > 0:
        free = [i for i in range(count - 1) if holding[i] < limit]
        pool, remaining = sum([weights[i] for i in free]), spare
        for i in free:
            more = min(limit - holding[i], max(1, remaining * weights[i] // pool), spare)
            holding[i] = holding[i] + more
            spare = spare - more
    return np.array([limit] + holding)


def ragged_sizes(own_key, count, total, most, slope):
    if count == 2:
        one = jax.random.randint(own_key, (), max(1, total - most), min(most, total - 1) + 1)
        return jnp.stack([one, total - one])
    sizes = jnp.asarray(length_profile(count, total, most, slope), jnp.int32)
    pairs = (count - 1) // 2
    giver, sink = sizes[1:1 + 2 * pairs:2], sizes[2:2 + 2 * pairs:2]
    margin = jnp.minimum(giver - 1, most - sink)
    passed = jax.random.randint(jax.random.fold_in(own_key, 1), (pairs,), 0, 1 << 20) % (margin + 1)
    sizes = sizes.at[1:1 + 2 * pairs:2].set(giver - passed).at[2:2 + 2 * pairs:2].set(sink + passed)
    return sizes[jax.random.permutation(jax.random.fold_in(own_key, 2), count)]


def bell_draw(own_key, dims, width, most, cuts=(), held_as=jnp.bfloat16):
    entries = jax.random.normal(own_key, dims, jnp.float32) * width
    if len(cuts) > 0:
        entries = level_of(own_key, dims, cuts, -0.22, 0.18) * entries
    return jnp.clip(entries, min=-most, max=most).astype(held_as)


def setup_inputs(seed: int = 0) -> dict:
    key_list = jax.random.split(jax.random.key(seed), 8)
    return {
        "queries": draw_queries(jax.random.fold_in(key_list[7], 71), 0),
        "suffix_kv": draw_suffix_kv(jax.random.fold_in(key_list[7], 71), 0),
        "prefix_key_value": bell_draw(key_list[2], (TOTAL_TILE_COUNT, TILE_TOKENS, 2 * KEY_VALUE_HEADS * HEAD_WIDTH), 1.0, 5.0, ((0, 32), (2, 8))),
        "answer_ids": jax.vmap(lambda own: jnp.searchsorted(jnp.cumsum(ragged_sizes(own, ANS_DEV, T_DEV, 2 * T_DEV // ANS_DEV, 2)), jnp.arange(T_DEV), side="right"))(jax.random.split(key_list[3], N_DP)).reshape((N_DP, T_DEV)).astype(jnp.int32),
        "read_tiles": draw_read_tiles(jax.random.fold_in(key_list[7], 71), 0),
        "visible": touch_ends((jax.random.randint(key_list[5], (N_DP, QG, READ_TILE_COUNT), 0, 4) < 3).astype(jnp.int32), jax.random.fold_in(key_list[5], 1), 0, 1),
        "out_weight": bell_draw(key_list[6], (QUERY_HEADS * HEAD_WIDTH, D_OUT), (QUERY_HEADS * HEAD_WIDTH // 8) ** -0.5, 0.1875, ((0, 8), (1, 32))),
    }


def head_attention(head_query, head_keys, head_values, visible_keys):
    scores = jnp.dot(head_query, head_keys.T, preferred_element_type=jnp.float32) * (HEAD_WIDTH ** -0.5)
    scores = jnp.where(visible_keys, scores, -jnp.inf)
    row_max = jnp.max(scores, axis=1, keepdims=True)
    exponent = jnp.exp(scores - row_max)
    row_total = jnp.sum(exponent, axis=1, keepdims=True)
    weights = exponent.astype(jnp.bfloat16)
    mixed = jnp.dot(weights, head_values, preferred_element_type=jnp.float32)
    return (mixed / row_total).astype(jnp.bfloat16)


def attend_group(query_rows, trailing_rows, gathered_tiles, answer_of, seen_table):
    question_of = answer_of * QG // ANS_DEV
    seen = seen_table[question_of] > 0
    prefix_mask = jnp.repeat(seen, TILE_TOKENS, axis=1)
    position = jnp.arange(T_DEV, dtype=jnp.int32)
    suffix_mask = (answer_of[:, None] == answer_of[None, :]) & (position[:, None] >= position[None, :])
    visible_keys = jnp.concatenate([prefix_mask, suffix_mask], axis=1)
    key_value_pairs = jnp.concatenate([gathered_tiles.reshape(READ_TILE_COUNT * TILE_TOKENS, 2 * KEY_VALUE_HEADS * HEAD_WIDTH), trailing_rows], axis=0)
    key_value_pairs = key_value_pairs.reshape(-1, KEY_VALUE_HEADS, 2, HEAD_WIDTH)
    per_head = query_rows.reshape(T_DEV, QUERY_HEADS, HEAD_WIDTH)
    heads_per_group = QUERY_HEADS // KEY_VALUE_HEADS

    def one_head(head_index):
        head_query = lax.dynamic_index_in_dim(per_head, head_index, 1, keepdims=False)
        key_value = lax.dynamic_index_in_dim(key_value_pairs, head_index // heads_per_group, 1, keepdims=False)
        return head_attention(head_query, key_value[:, 0], key_value[:, 1], visible_keys)

    heads_out = lax.map(one_head, jnp.arange(QUERY_HEADS, dtype=jnp.int32))
    return heads_out.transpose(1, 0, 2).reshape(T_DEV, QUERY_HEADS * HEAD_WIDTH)


def reference(queries, suffix_kv, prefix_key_value, answer_ids, read_tiles, visible, out_weight):
    def per_group(group_index):
        row_start = (group_index * T_DEV).astype(jnp.int32)
        query_rows = lax.dynamic_slice_in_dim(queries, row_start, T_DEV, 0)
        trailing_rows = lax.dynamic_slice_in_dim(suffix_kv, row_start, T_DEV, 0)
        gathered_tiles = jnp.take(prefix_key_value, read_tiles[group_index], axis=0)
        return attend_group(query_rows, trailing_rows, gathered_tiles, answer_ids[group_index], visible[group_index])

    attended = lax.map(per_group, jnp.arange(N_DP, dtype=jnp.int32))
    attended = attended.reshape(ANSWER_TOKENS, QUERY_HEADS * HEAD_WIDTH)
    return jnp.dot(attended, out_weight, preferred_element_type=jnp.float32).astype(jnp.bfloat16)
```

```python
import functools

import jax
import jax.numpy as jnp
from jax import lax
from jax.experimental import pallas as pl
from jax.experimental.pallas import tpu as pltpu
from jax.sharding import PartitionSpec as P

HEAD = 128
TILE = 64
READS = 26
GROUPS = 32
TPS = 8
TOK = 512
HEADS = 8
BLK = 128
NBLK = TOK // BLK
PRE = READS * TILE
KEYS = PRE + 2 * BLK
NZ = 8
COLS = 512
MESH = pl.DeviceIdType.MESH
BIG = -1e30
LOG2E = 1.4426950408889634
SCALE = HEAD ** (-0.5) * LOG2E


def coords():
    g = lax.axis_index("dp")
    return g // 8, lax.rem(g // 2, 4), lax.rem(g, 2), lax.axis_index("tensor")


def place(x, y, c):
    return lax.rem(x, 4) * 8 + lax.rem(y, 4) * 2 + lax.rem(c, 2)


def remote(src, dst, send, recv, dp, tensor):
    return pltpu.make_async_remote_copy(
        src_ref=src, dst_ref=dst, send_sem=send, recv_sem=recv,
        device_id=(dp, tensor), device_id_type=MESH,
    )


def fetch_kernel(reads, prefix, keys, values, ask, table, asked, packed, got,
                 hot_out, sem_send, sem_recv, hot_recv, spread_send, spread_recv, local_sem):
    x, y, c, z = coords()
    me = lax.axis_index("dp")
    peers = [place(x + k // 8, y + (k // 2) % 4, c + k % 2) for k in range(1, GROUPS)]
    barrier = pltpu.get_barrier_semaphore()
    for peer in peers:
        pl.semaphore_signal(barrier, inc=1, device_id=(peer, z), device_id_type=MESH)

    lane = lax.broadcasted_iota(jnp.int32, (1, 128), 1)
    first = jnp.full((1, 128), TPS, jnp.int32)
    last = jnp.full((1, 128), -1, jnp.int32)
    tiles = [reads[0, r] for r in range(READS)]
    for tile in tiles:
        here = lane == tile // TPS
        first = jnp.where(here, jnp.minimum(first, tile % TPS), first)
        last = jnp.where(here, jnp.maximum(last, tile % TPS), last)
    twice = last > first
    hot_owner = jnp.max(jnp.where(twice, lane, 0))
    hot_second = jnp.max(jnp.where(twice, last, 0))
    mine = jnp.where(first == TPS, 0, first)
    ask[...] = mine
    table[pl.ds(me, 1)] = mine[None]
    second = prefix[hot_second]
    hot_out[pl.ds(0, TILE)] = second[:, :HEAD]
    hot_out[pl.ds(TILE, TILE)] = second[:, HEAD:]

    pl.semaphore_wait(barrier, GROUPS - 1)
    for peer in peers:
        remote(ask, table.at[me], sem_send.at[0], sem_recv.at[0], peer, z).start()
    for peer in peers:
        part = pl.multiple_of(lax.rem(peer, 8) * 16, 16)
        remote(hot_out.at[pl.ds(part, 16)], hot_recv.at[me],
               sem_send.at[1], sem_recv.at[1], peer, z).start()
    my_part = pl.multiple_of(lax.rem(me, 8) * 16, 16)
    hot_recv[pl.ds(me, 1)] = hot_out[pl.ds(my_part, 16)][None]

    others = table.at[pl.ds(0, GROUPS - 1)]
    pltpu.make_async_copy(others, others, sem_recv.at[0]).wait()
    load = pltpu.make_async_copy(table, asked, local_sem)
    load.start()
    load.wait()
    for k, peer in enumerate(peers):
        tile = prefix[asked[peer, 0, me]]
        packed[k, pl.ds(0, TILE)] = tile[:, :HEAD]
        packed[k, pl.ds(TILE, TILE)] = tile[:, HEAD:]
        remote(packed.at[k], got.at[me], sem_send.at[2], sem_recv.at[2], peer, z).start()
    own = prefix[asked[me, 0, me]]
    got[pl.ds(me, 1), pl.ds(0, TILE)] = own[:, :HEAD][None]
    got[pl.ds(me, 1), pl.ds(TILE, TILE)] = own[:, HEAD:][None]

    others = hot_recv.at[pl.ds(0, GROUPS - 1)]
    pltpu.make_async_copy(others, others, sem_recv.at[1]).wait()
    piece = hot_recv[hot_owner]
    got[GROUPS, pl.ds(my_part, 16)] = piece
    spread = []
    for k in range(1, 8):
        peer = place(x, y + k // 2, c + k % 2)
        copy = remote(got.at[GROUPS, pl.ds(my_part, 16)], got.at[GROUPS, pl.ds(my_part, 16)],
                      spread_send.at[k], spread_recv.at[k], peer, z)
        copy.start()
        spread.append(copy)

    others = got.at[pl.ds(0, GROUPS - 1)]
    pltpu.make_async_copy(others, others, sem_recv.at[2]).wait()
    for copy in spread:
        copy.wait_recv()
    for r, tile in enumerate(tiles):
        owner = tile // TPS
        from_second = (owner == hot_owner) & (tile % TPS == hot_second)
        block = got[jnp.where(from_second, GROUPS, owner)]
        keys[pl.ds(r * TILE, TILE)] = block[:TILE]
        values[pl.ds(r * TILE, TILE)] = block[TILE:]
    for ref, sem in ((table.at[pl.ds(0, GROUPS - 1)], sem_send.at[0]),
                     (hot_recv.at[pl.ds(0, GROUPS - 1)], sem_send.at[1]),
                     (packed, sem_send.at[2])):
        pltpu.make_async_copy(ref, ref, sem).wait()
    for copy in spread:
        copy.wait_send()


def fetch(reads, prefix):
    half = jax.ShapeDtypeStruct((PRE, HEAD), jnp.bfloat16)
    vmem = pl.BlockSpec(memory_space=pltpu.VMEM)
    return pl.pallas_call(
        fetch_kernel,
        out_shape=(half, half),
        in_specs=[pl.BlockSpec(memory_space=pltpu.SMEM), vmem],
        out_specs=(vmem, vmem),
        scratch_shapes=[
            pltpu.VMEM((1, 128), jnp.int32),
            pltpu.VMEM((GROUPS, 1, 128), jnp.int32),
            pltpu.SMEM((GROUPS, 1, 128), jnp.int32),
            pltpu.VMEM((GROUPS - 1, 2 * TILE, HEAD), jnp.bfloat16),
            pltpu.VMEM((GROUPS + 1, 2 * TILE, HEAD), jnp.bfloat16),
            pltpu.VMEM((2 * TILE, HEAD), jnp.bfloat16),
            pltpu.SemaphoreType.DMA((3,)),
            pltpu.SemaphoreType.DMA((3,)),
            pltpu.VMEM((GROUPS, 16, HEAD), jnp.bfloat16),
            pltpu.SemaphoreType.DMA((8,)),
            pltpu.SemaphoreType.DMA((8,)),
            pltpu.SemaphoreType.DMA,
        ],
        name="fetch_tiles",
        compiler_params=pltpu.CompilerParams(
            collective_id=0, has_side_effects=True, vmem_limit_bytes=16 << 20
        ),
    )(reads, prefix)


RING = (0, 3, 1, 2)


class Weights:
    def __init__(self, own, blocks, send, recv):
        self.own, self.blocks, self.send, self.recv = own, blocks, send, recv
        self.x, self.y, self.c, self.z = coords()
        self.started = []

    def at(self, f, s, other=False):
        c = 1 - self.c if other else self.c
        x = self.x + f * (1 - c) + s * c
        y = self.y + s * (1 - c) + f * c
        return place(x, y, c)

    def copy(self, kind, block, dp, rows=None, src=None):
        ref = self.blocks.at[block]
        if rows is not None:
            ref = ref.at[pl.ds(rows * 512, 512)]
        return remote(ref if src is None else src, ref, self.send.at[kind],
                      self.recv.at[kind], dp, self.z)

    def go(self, *args, **kw):
        copy = self.copy(*args, **kw)
        copy.start()
        self.started.append(copy)

    def to_sibling(self, jf, js, src=None):
        self.go(20 + 4 * jf + js, self.at(RING[jf], RING[js]),
                place(self.x, self.y, self.c + 1), src=src)

    def neighbours(self):
        return [self.at(1, 0), self.at(3, 0), self.at(0, 1), self.at(0, 3),
                place(self.x, self.y, self.c + 1)]

    def start(self):
        me = self.at(0, 0)
        self.go(0, me, self.at(1, 0), src=self.own)
        self.go(1, me, self.at(3, 0), src=self.own)
        self.go(4, me, self.at(0, 1), src=self.own)
        self.go(5, me, self.at(0, 3), src=self.own)
        self.to_sibling(0, 0, src=self.own)
        self.blocks[pl.ds(me, 1)] = self.own[...][None]

    def first_axis(self):
        me = self.at(0, 0)
        before, after = self.at(3, 0), self.at(1, 0)
        self.copy(0, before, me).wait_recv()
        self.go(2, before, after, rows=0)
        self.go(6, before, self.at(0, 1))
        self.go(7, before, self.at(0, 3))
        self.copy(1, after, me).wait_recv()
        self.go(3, after, before, rows=1)
        self.go(8, after, self.at(0, 1))
        self.go(9, after, self.at(0, 3))
        self.to_sibling(1, 0)
        self.to_sibling(2, 0)

    def opposite(self):
        me = self.at(0, 0)
        far = self.at(2, 0)
        self.copy(2, far, me, rows=0).wait_recv()
        self.copy(3, far, me, rows=1).wait_recv()
        self.go(10, far, self.at(0, 1))
        self.go(11, far, self.at(0, 3))
        self.to_sibling(3, 0)

    def second_axis(self, jf):
        me = self.at(0, 0)
        before, after = self.at(RING[jf], 3), self.at(RING[jf], 1)
        self.copy(4 + 2 * jf, before, me).wait_recv()
        self.go(12 + 2 * jf, before, self.at(0, 1), rows=0)
        self.copy(5 + 2 * jf, after, me).wait_recv()
        self.go(13 + 2 * jf, after, self.at(0, 3), rows=1)
        self.to_sibling(jf, 1)
        self.to_sibling(jf, 2)

    def last(self, jf):
        me = self.at(0, 0)
        far = self.at(RING[jf], 2)
        self.copy(12 + 2 * jf, far, me, rows=0).wait_recv()
        self.copy(13 + 2 * jf, far, me, rows=1).wait_recv()
        self.to_sibling(jf, 3)

    def finish(self):
        me = self.at(0, 0)
        for jf in range(4):
            for js in range(4):
                block = self.at(RING[jf], RING[js], other=True)
                self.copy(20 + 4 * jf + js, block, me).wait_recv()

    def drain(self):
        for copy in self.started:
            copy.wait_send()


def layer_kernel(visible, q, suffix, pre_k, pre_v, ids, w, out,
                 blocks, ka, va, qa, att, to_right, to_left, at_right, at_left,
                 w_send, w_recv, r_send, r_recv, l_send, l_recv):
    x, y, c, z = coords()
    me = lax.axis_index("dp")
    right, left = lax.rem(z + 1, NZ), lax.rem(z + NZ - 1, NZ)
    weights = Weights(w, blocks, w_send, w_recv)
    barrier = pltpu.get_barrier_semaphore()
    for peer in weights.neighbours():
        pl.semaphore_signal(barrier, inc=1, device_id=(peer, z), device_id_type=MESH)
    pl.semaphore_signal(barrier, inc=1, device_id=(me, right), device_id_type=MESH)
    pl.semaphore_signal(barrier, inc=1, device_id=(me, left), device_id_type=MESH)
    pl.semaphore_wait(barrier, 7)
    weights.start()

    ka[pl.ds(0, PRE), pl.ds(0, HEAD)] = pre_k[...]
    va[pl.ds(0, PRE), pl.ds(0, HEAD)] = pre_v[...]
    va[:, pl.ds(HEAD, HEAD)] = jnp.ones((KEYS, HEAD), jnp.bfloat16)
    row = lax.broadcasted_iota(jnp.int32, (BLK, BLK), 0)
    col = lax.broadcasted_iota(jnp.int32, (BLK, BLK), 1)
    qa[:, pl.ds(HEAD, HEAD)] = jnp.where(row == col, 1.0, 0.0).astype(jnp.bfloat16)

    def attend(b):
        token_ids = ids[:, pl.ds(b * BLK, BLK)]
        second = token_ids * 2 // 16 == 1
        for r in range(READS):
            zero = jnp.where(visible[0, 0, r] > 0, 0.0, BIG)
            one = jnp.where(visible[0, 1, r] > 0, 0.0, BIG)
            bias = jnp.where(second, one, zero)
            ka[pl.ds(r * TILE, TILE), pl.ds(HEAD, HEAD)] = jnp.broadcast_to(
                bias, (TILE, BLK)).astype(jnp.bfloat16)
        start = max(b - 1, 0) * BLK
        for part in range(2):
            base = start + part * BLK
            at = PRE + part * BLK
            key_ids = jnp.broadcast_to(
                ids[:, pl.ds(base, BLK)].astype(jnp.float32), (BLK, BLK)).T
            same = key_ids == token_ids.astype(jnp.float32)
            seen = same & (row + base <= col + b * BLK)
            ka[pl.ds(at, BLK), pl.ds(0, HEAD)] = suffix[pl.ds(base, BLK), pl.ds(0, HEAD)]
            ka[pl.ds(at, BLK), pl.ds(HEAD, HEAD)] = jnp.where(seen, 0.0, BIG).astype(jnp.bfloat16)
            va[pl.ds(at, BLK), pl.ds(0, HEAD)] = suffix[pl.ds(base, BLK), pl.ds(HEAD, HEAD)]

        def head(h, _):
            lanes = pl.ds(pl.multiple_of(h * HEAD, HEAD), HEAD)
            qa[:, pl.ds(0, HEAD)] = q[pl.ds(b * BLK, BLK), lanes]
            scores = lax.dot_general(qa[...], ka[...], (((1,), (1,)), ((), ())),
                                     preferred_element_type=jnp.float32)
            top = jnp.max(scores, axis=1, keepdims=True)
            probs = jnp.exp2((scores - top) * SCALE).astype(jnp.bfloat16)
            mixed = jnp.dot(probs, va[...], preferred_element_type=jnp.float32)
            att[pl.ds(b * BLK, BLK), lanes] = (
                mixed[:, :HEAD] / mixed[:, HEAD:]).astype(jnp.bfloat16)
            return 0

        lax.fori_loop(0, HEADS, head, 0)

    attend(0)
    weights.first_axis()
    attend(1)
    weights.opposite()
    weights.second_axis(0)
    attend(2)
    weights.second_axis(1)
    weights.second_axis(2)
    attend(3)
    weights.last(0)
    weights.second_axis(3)
    for jf in range(1, 4):
        weights.last(jf)
    weights.finish()

    def project(b, dest):
        base = lax.rem(dest, NZ) * 4
        wide = jnp.concatenate([blocks[base + i] for i in range(4)], axis=1)
        rows = pl.ds(pl.multiple_of(b * BLK, BLK), BLK)
        return jnp.dot(att[rows, :], wide, preferred_element_type=jnp.float32)

    half = COLS // 2

    def send(k, b, to, at, sems, peer):
        rows = pl.ds(pl.multiple_of(b * BLK, BLK), BLK)
        width = half if k == 4 else COLS
        return remote(to.at[k - 1, rows, pl.ds(0, width)], at.at[k - 1, rows, pl.ds(0, width)],
                      sems[0].at[k - 1, b], sems[1].at[k - 1, b], me, peer)

    def go_right(k, b):
        return send(k, b, to_right, at_right, (r_send, r_recv), right)

    def go_left(k, b):
        return send(k, b, to_left, at_left, (l_send, l_recv), left)

    def store(ref, k, b, value):
        rows = pl.ds(pl.multiple_of(b * BLK, BLK), BLK)
        ref[k - 1, rows, pl.ds(0, value.shape[1])] = value.astype(jnp.bfloat16)

    def arrived(ref, k, b):
        rows = pl.ds(pl.multiple_of(b * BLK, BLK), BLK)
        width = half if k == 3 else COLS
        return ref[k, rows, pl.ds(0, width)].astype(jnp.float32)

    def stage4(b, _):
        part = project(b, z + 4)
        store(to_right, 4, b, part[:, :half])
        go_right(4, b).start()
        store(to_left, 4, b, part[:, half:])
        go_left(4, b).start()
        return 0

    def stage3(b, _):
        part = project(b, z + 3)
        go_right(4, b).wait_recv()
        store(to_right, 3, b, jnp.concatenate(
            [part[:, :half] + arrived(at_right, 3, b), part[:, half:]], axis=1))
        go_right(3, b).start()
        part = project(b, z + 5)
        go_left(4, b).wait_recv()
        store(to_left, 3, b, jnp.concatenate(
            [part[:, :half], part[:, half:] + arrived(at_left, 3, b)], axis=1))
        go_left(3, b).start()
        return 0

    def stage(k):
        def body(b, _):
            part = project(b, z + k)
            go_right(k + 1, b).wait_recv()
            store(to_right, k, b, part + arrived(at_right, k, b))
            go_right(k, b).start()
            part = project(b, z + NZ - k)
            go_left(k + 1, b).wait_recv()
            store(to_left, k, b, part + arrived(at_left, k, b))
            go_left(k, b).start()
            return 0
        return body

    def final(b, _):
        part = project(b, z)
        go_right(1, b).wait_recv()
        part = part + arrived(at_right, 0, b)
        go_left(1, b).wait_recv()
        part = part + arrived(at_left, 0, b)
        rows = pl.ds(pl.multiple_of(b * BLK, BLK), BLK)
        out[rows, :] = part.astype(jnp.bfloat16)
        return 0

    for body in (stage4, stage3, stage(2), stage(1), final):
        lax.fori_loop(0, NBLK, body, 0)

    def drain(b, _):
        for k in range(1, 5):
            go_right(k, b).wait_send()
            go_left(k, b).wait_send()
        return 0

    lax.fori_loop(0, NBLK, drain, 0)
    weights.drain()


def layer(visible, q, suffix, pre_k, pre_v, ids, w):
    vmem = pl.BlockSpec(memory_space=pltpu.VMEM)
    bf16 = jnp.bfloat16
    return pl.pallas_call(
        layer_kernel,
        out_shape=jax.ShapeDtypeStruct((TOK, COLS), bf16),
        in_specs=[pl.BlockSpec(memory_space=pltpu.SMEM)] + [vmem] * 6,
        out_specs=vmem,
        scratch_shapes=[
            pltpu.VMEM((GROUPS, HEADS * HEAD, HEAD), bf16),
            pltpu.VMEM((KEYS, 2 * HEAD), bf16),
            pltpu.VMEM((KEYS, 2 * HEAD), bf16),
            pltpu.VMEM((BLK, 2 * HEAD), bf16),
            pltpu.VMEM((TOK, HEADS * HEAD), bf16),
            pltpu.VMEM((4, TOK, COLS), bf16),
            pltpu.VMEM((4, TOK, COLS), bf16),
            pltpu.VMEM((4, TOK, COLS), bf16),
            pltpu.VMEM((4, TOK, COLS), bf16),
            pltpu.SemaphoreType.DMA((36,)),
            pltpu.SemaphoreType.DMA((36,)),
            pltpu.SemaphoreType.DMA((4, NBLK)),
            pltpu.SemaphoreType.DMA((4, NBLK)),
            pltpu.SemaphoreType.DMA((4, NBLK)),
            pltpu.SemaphoreType.DMA((4, NBLK)),
        ],
        name="attend_project_reduce",
        compiler_params=pltpu.CompilerParams(
            collective_id=1, has_side_effects=True, vmem_limit_bytes=52 << 20
        ),
    )(visible, q, suffix, pre_k, pre_v, ids, w)


def local(queries, suffix_kv, prefix_key_value, answer_ids, read_tiles, visible, out_weight):
    pre_k, pre_v = fetch(read_tiles, prefix_key_value)
    return layer(visible, queries, suffix_kv, pre_k, pre_v, answer_ids, out_weight)


def solution(mesh):
    placed = (
        P("dp", "tensor"),
        P("dp", "tensor"),
        P("dp", None, "tensor"),
        P("dp", None),
        P("dp", None),
        P("dp", None, None),
        P("tensor", "dp"),
    )
    return jax.shard_map(
        local, mesh=mesh, in_specs=placed, out_specs=P("dp", "tensor"), check_vma=False
    )
```

```python
import functools

import jax
import jax.numpy as jnp
from jax import lax
from jax.experimental import pallas as pl
from jax.experimental.pallas import tpu as pltpu
from jax.sharding import PartitionSpec as P

HEAD = 128
TILE = 64
READS = 26
GROUPS = 32
TPS = 8
TOK = 512
HEADS = 8
BLK = 128
NBLK = TOK // BLK
PRE = READS * TILE
KEYS = PRE + 2 * BLK
NZ = 8
COLS = 512
MESH = pl.DeviceIdType.MESH
PAIR = 2 * BLK
BF16 = jnp.bfloat16
F32 = jnp.float32
BIG = -1e30
LOG2E = 1.4426950408889634
SCALE = HEAD ** (-0.5) * LOG2E


def coords():
    g = lax.axis_index("dp")
    return g // 8, lax.rem(g // 2, 4), lax.rem(g, 2), lax.axis_index("tensor")


def place(x, y, c):
    return lax.rem(x, 4) * 8 + lax.rem(y, 4) * 2 + lax.rem(c, 2)


def remote(src, dst, send, recv, dp, tensor):
    return pltpu.make_async_remote_copy(
        src_ref=src, dst_ref=dst, send_sem=send, recv_sem=recv,
        device_id=(dp, tensor), device_id_type=MESH,
    )


class Tiles:
    def __init__(self, reads, prefix, ask, table, asked, packed, got, hot_out, hot_recv,
                 sem_send, sem_recv, spread_send, spread_recv, local_sem):
        self.reads, self.prefix, self.ask, self.table, self.asked = reads, prefix, ask, table, asked
        self.packed, self.got, self.hot_out, self.hot_recv = packed, got, hot_out, hot_recv
        self.sem_send, self.sem_recv, self.local_sem = sem_send, sem_recv, local_sem
        self.spread_send, self.spread_recv = spread_send, spread_recv
        self.x, self.y, self.c, self.z = coords()
        self.me = lax.axis_index("dp")
        self.peers = [place(self.x + k // 8, self.y + (k // 2) % 4, self.c + k % 2)
                      for k in range(1, GROUPS)]

    def plan(self):
        lane = lax.broadcasted_iota(jnp.int32, (1, 128), 1)
        first = jnp.full((1, 128), TPS, jnp.int32)
        last = jnp.full((1, 128), -1, jnp.int32)
        self.tiles = [self.reads[0, r] for r in range(READS)]
        for tile in self.tiles:
            here = lane == tile // TPS
            first = jnp.where(here, jnp.minimum(first, tile % TPS), first)
            last = jnp.where(here, jnp.maximum(last, tile % TPS), last)
        twice = last > first
        self.hot_owner = jnp.max(jnp.where(twice, lane, 0))
        self.hot_second = jnp.max(jnp.where(twice, last, 0))
        mine = jnp.where(first == TPS, 0, first)
        self.ask[...] = mine
        self.table[pl.ds(self.me, 1)] = mine[None]

    def cut(self):
        second = self.prefix[self.hot_second]
        self.hot_out[pl.ds(0, TILE)] = second[:, :HEAD]
        self.hot_out[pl.ds(TILE, TILE)] = second[:, HEAD:]
        self.part = pl.multiple_of(lax.rem(self.me, 8) * 16, 16)
        self.hot_recv[pl.ds(self.me, 1)] = self.hot_out[pl.ds(self.part, 16)][None]

    def request(self):
        for peer in self.peers:
            remote(self.ask, self.table.at[self.me], self.sem_send.at[0], self.sem_recv.at[0],
                   peer, self.z).start()

    def pieces(self):
        for peer in self.peers:
            part = pl.multiple_of(lax.rem(peer, 8) * 16, 16)
            remote(self.hot_out.at[pl.ds(part, 16)], self.hot_recv.at[self.me],
                   self.sem_send.at[1], self.sem_recv.at[1], peer, self.z).start()

    def wait_all(self, ref, sem):
        part = ref.at[pl.ds(0, GROUPS - 1)]
        pltpu.make_async_copy(part, part, sem).wait()

    def answer(self):
        me, z = self.me, self.z
        self.wait_all(self.table, self.sem_recv.at[0])
        load = pltpu.make_async_copy(self.table, self.asked, self.local_sem)
        load.start()
        load.wait()
        for k, peer in enumerate(self.peers):
            tile = self.prefix[self.asked[peer, 0, me]]
            self.packed[k, pl.ds(0, TILE)] = tile[:, :HEAD]
            self.packed[k, pl.ds(TILE, TILE)] = tile[:, HEAD:]
            remote(self.packed.at[k], self.got.at[me], self.sem_send.at[2],
                   self.sem_recv.at[2], peer, z).start()
        own = self.prefix[self.asked[me, 0, me]]
        self.got[pl.ds(me, 1), pl.ds(0, TILE)] = own[:, :HEAD][None]
        self.got[pl.ds(me, 1), pl.ds(TILE, TILE)] = own[:, HEAD:][None]

    def spread(self):
        self.wait_all(self.hot_recv, self.sem_recv.at[1])
        ref = self.got.at[GROUPS, pl.ds(self.part, 16)]
        self.got[GROUPS, pl.ds(self.part, 16)] = self.hot_recv[self.hot_owner]
        self.spreads = []
        for k in range(1, 8):
            copy = remote(ref, ref, self.spread_send.at[k], self.spread_recv.at[k],
                          place(self.x, self.y + k // 2, self.c + k % 2), self.z)
            copy.start()
            self.spreads.append(copy)

    def receive(self):
        self.wait_all(self.got, self.sem_recv.at[2])
        for copy in self.spreads:
            copy.wait_recv()

    def tile(self, r):
        owner = self.tiles[r] // TPS
        second = (owner == self.hot_owner) & (self.tiles[r] % TPS == self.hot_second)
        return self.got[jnp.where(second, GROUPS, owner)]

    def drain(self):
        self.wait_all(self.table, self.sem_send.at[0])
        self.wait_all(self.hot_recv, self.sem_send.at[1])
        self.wait_all(self.packed, self.sem_send.at[2])
        for copy in self.spreads:
            copy.wait_send()


RING = (0, 3, 1, 2)


class Weights:
    def __init__(self, blocks, send, recv):
        self.blocks, self.send, self.recv = blocks, send, recv
        self.x, self.y, self.c, self.z = coords()
        self.started = []

    def at(self, f, s, other=False):
        c = 1 - self.c if other else self.c
        x = self.x + f * (1 - c) + s * c
        y = self.y + s * (1 - c) + f * c
        return place(x, y, c)

    def copy(self, kind, block, dp, rows=None):
        ref = self.blocks.at[block]
        if rows is not None:
            ref = ref.at[pl.ds(rows * 512, 512)]
        return remote(ref, ref, self.send.at[kind], self.recv.at[kind], dp, self.z)

    def go(self, *args, **kw):
        copy = self.copy(*args, **kw)
        copy.start()
        self.started.append(copy)

    def to_sibling(self, jf, js):
        self.go(20 + 4 * jf + js, self.at(RING[jf], RING[js]),
                place(self.x, self.y, self.c + 1))

    def start(self):
        me = self.at(0, 0)
        self.go(0, me, self.at(1, 0))
        self.go(1, me, self.at(3, 0))
        self.go(4, me, self.at(0, 1))
        self.go(5, me, self.at(0, 3))
        self.to_sibling(0, 0)

    def first_axis(self):
        me = self.at(0, 0)
        before, after = self.at(3, 0), self.at(1, 0)
        self.copy(0, before, me).wait_recv()
        self.go(2, before, after, rows=0)
        self.go(6, before, self.at(0, 1))
        self.go(7, before, self.at(0, 3))
        self.copy(1, after, me).wait_recv()
        self.go(3, after, before, rows=1)
        self.go(8, after, self.at(0, 1))
        self.go(9, after, self.at(0, 3))
        self.to_sibling(1, 0)
        self.to_sibling(2, 0)

    def opposite(self):
        me = self.at(0, 0)
        far = self.at(2, 0)
        self.copy(2, far, me, rows=0).wait_recv()
        self.copy(3, far, me, rows=1).wait_recv()
        self.go(10, far, self.at(0, 1))
        self.go(11, far, self.at(0, 3))
        self.to_sibling(3, 0)

    def second_axis(self, jf):
        me = self.at(0, 0)
        before, after = self.at(RING[jf], 3), self.at(RING[jf], 1)
        self.copy(4 + 2 * jf, before, me).wait_recv()
        self.go(12 + 2 * jf, before, self.at(0, 1), rows=0)
        self.copy(5 + 2 * jf, after, me).wait_recv()
        self.go(13 + 2 * jf, after, self.at(0, 3), rows=1)
        self.to_sibling(jf, 1)
        self.to_sibling(jf, 2)

    def last(self, jf):
        me = self.at(0, 0)
        far = self.at(RING[jf], 2)
        self.copy(12 + 2 * jf, far, me, rows=0).wait_recv()
        self.copy(13 + 2 * jf, far, me, rows=1).wait_recv()
        self.to_sibling(jf, 3)

    def finish(self):
        me = self.at(0, 0)
        for jf in range(4):
            for js in range(4):
                block = self.at(RING[jf], RING[js], other=True)
                self.copy(20 + 4 * jf + js, block, me).wait_recv()

    def drain(self):
        for copy in self.started:
            copy.wait_send()


class Reduce:
    def __init__(self, att, blocks, out, to_right, to_left, at_right, at_left,
                 r_send, r_recv, l_send, l_recv):
        self.att, self.blocks, self.out = att, blocks, out
        self.me, self.z = lax.axis_index("dp"), lax.axis_index("tensor")
        right, left = lax.rem(self.z + 1, NZ), lax.rem(self.z + NZ - 1, NZ)
        self.right = (to_right, at_right, r_send, r_recv, right)
        self.left = (to_left, at_left, l_send, l_recv, left)

    def rows(self, b):
        return pl.ds(pl.multiple_of(b * BLK, BLK), BLK)

    def project(self, b, hops):
        base = lax.rem(self.z + NZ + hops, NZ) * 4
        wide = jnp.concatenate([self.blocks[base + i] for i in range(4)], axis=1)
        return jnp.dot(self.att[self.rows(b), :], wide, preferred_element_type=F32)

    def copy(self, way, k, b):
        to, at, send, recv, peer = way
        part = (k - 1, self.rows(b), pl.ds(0, COLS // 2 if k == 4 else COLS))
        return remote(to.at[part], at.at[part], send.at[k - 1, b], recv.at[k - 1, b],
                      self.me, peer)

    def send(self, way, k, b, value):
        way[0][k - 1, self.rows(b), pl.ds(0, value.shape[1])] = value.astype(BF16)
        self.copy(way, k, b).start()

    def arrived(self, way, k, b):
        self.copy(way, k + 1, b).wait_recv()
        return way[1][k, self.rows(b), pl.ds(0, COLS // 2 if k == 3 else COLS)].astype(F32)

    def stage(self, k):
        half = COLS // 2

        def body(b, _):
            if k == 4:
                part = self.project(b, 4)
                self.send(self.right, 4, b, part[:, :half])
                self.send(self.left, 4, b, part[:, half:])
            elif k == 0:
                part = self.project(b, 0)
                part = part + self.arrived(self.right, 0, b)
                part = part + self.arrived(self.left, 0, b)
                self.out[self.rows(b), :] = part.astype(BF16)
            else:
                for way, hops in ((self.right, k), (self.left, -k)):
                    part = self.project(b, hops)
                    come = self.arrived(way, k, b)
                    if k == 3 and hops > 0:
                        part = jnp.concatenate([part[:, :half] + come, part[:, half:]], axis=1)
                    elif k == 3:
                        part = jnp.concatenate([part[:, :half], part[:, half:] + come], axis=1)
                    else:
                        part = part + come
                    self.send(way, k, b, part)
            return 0

        lax.fori_loop(0, NBLK, body, 0)

    def drain(self):
        def body(b, _):
            for k in range(1, 5):
                self.copy(self.right, k, b).wait_send()
                self.copy(self.left, k, b).wait_send()
            return 0

        lax.fori_loop(0, NBLK, body, 0)


class Attention:
    def __init__(self, visible, ids, q, suffix, ka, va, qa, scores, att):
        self.visible, self.ids, self.q, self.suffix = visible, ids, q, suffix
        self.ka, self.va, self.qa, self.scores, self.att = ka, va, qa, scores, att

    def fixed(self):
        row = lax.broadcasted_iota(jnp.int32, (BLK, BLK), 0)
        col = lax.broadcasted_iota(jnp.int32, (BLK, BLK), 1)
        self.row, self.col = row, col
        eye = jnp.where(row == col, 1.0, 0.0).astype(BF16)
        for slot in range(2):
            for j in range(2):
                self.qa[slot, pl.ds(j * BLK, BLK), pl.ds(HEAD, HEAD)] = eye
            self.va[slot, :, pl.ds(HEAD, HEAD)] = jnp.ones((KEYS, HEAD), BF16)
        self.down = [jnp.broadcast_to(self.ids[:, pl.ds(b * BLK, BLK)].astype(F32), (BLK, BLK)).T
                     for b in range(NBLK)]

    def bias(self, b):
        slot = b % 2
        second = self.down[b] >= 8.0
        for r in range(0, READS, 2):
            lines = [jnp.where(self.col < TILE,
                               jnp.where(self.visible[0, n, r] > 0, 0.0, BIG),
                               jnp.where(self.visible[0, n, r + 1] > 0, 0.0, BIG))
                     for n in range(2)]
            self.ka[slot, pl.ds(HEAD, HEAD), pl.ds(r * TILE, BLK)] = jnp.where(
                second, lines[1], lines[0]).astype(BF16)
        start = max(b - 1, 0) * BLK
        for part in range(2):
            base = start + part * BLK
            at = pl.ds(PRE + part * BLK, BLK)
            same = self.down[b] == self.ids[:, pl.ds(base, BLK)].astype(F32)
            seen = same & (self.col + base <= self.row + b * BLK)
            self.ka[slot, pl.ds(HEAD, HEAD), at] = jnp.where(seen, 0.0, BIG).astype(BF16)
            self.ka[slot, pl.ds(0, HEAD), at] = self.suffix[pl.ds(base, BLK), pl.ds(0, HEAD)].T
            self.va[slot, at, pl.ds(0, HEAD)] = self.suffix[pl.ds(base, BLK), pl.ds(HEAD, HEAD)]

    def take(self, tiles):
        for r in range(0, READS, 2):
            one, two = tiles.tile(r), tiles.tile(r + 1)
            across = jnp.concatenate([one[:TILE], two[:TILE]], axis=0).T
            for slot in range(2):
                self.ka[slot, pl.ds(0, HEAD), pl.ds(r * TILE, BLK)] = across
                self.va[slot, pl.ds(r * TILE, TILE), pl.ds(0, HEAD)] = one[TILE:]
                self.va[slot, pl.ds((r + 1) * TILE, TILE), pl.ds(0, HEAD)] = two[TILE:]

    def score(self, i):
        b, h = i // 4, i % 4 * 2
        for j in range(2):
            self.qa[i % 2, pl.ds(j * BLK, BLK), pl.ds(0, HEAD)] = (
                self.q[pl.ds(b * BLK, BLK), pl.ds((h + j) * HEAD, HEAD)])
        self.scores[i % 2] = jnp.dot(self.qa[i % 2], self.ka[b % 2], preferred_element_type=F32)

    def rest(self, i):
        b, h = i // 4, i % 4 * 2
        scores = self.scores[i % 2]
        top = jnp.max(scores, axis=1, keepdims=True)
        probs = jnp.exp2((scores - top) * SCALE).astype(BF16)
        mixed = jnp.dot(probs, self.va[b % 2], preferred_element_type=F32)
        done = (mixed[:, :HEAD] / mixed[:, HEAD:]).astype(BF16)
        for j in range(2):
            self.att[pl.ds(b * BLK, BLK), pl.ds((h + j) * HEAD, HEAD)] = done[j * BLK:(j + 1) * BLK]

    def block(self, b):
        for i in range(4 * b, 4 * b + 4):
            if i % 4 == 3 and b + 1 < NBLK:
                self.bias(b + 1)
            if i + 1 < 4 * NBLK:
                self.score(i + 1)
            self.rest(i)


def layer_kernel(reads, visible, prefix_hbm, q_hbm, suffix_hbm, ids, w_hbm, out,
                 prefix, q, suffix, load_sem, blocks, w_send, w_recv,
                 ask, table, asked, packed, got, hot_out, hot_recv,
                 t_send, t_recv, spread_send, spread_recv, local_sem,
                 ka, va, qa, scores, att,
                 to_right, to_left, at_right, at_left, r_send, r_recv, l_send, l_recv):
    me, z = lax.axis_index("dp"), lax.axis_index("tensor")
    loads = [pltpu.make_async_copy(src, dst, load_sem.at[i]) for i, (src, dst) in enumerate(
        ((prefix_hbm, prefix), (w_hbm, blocks.at[me]), (suffix_hbm, suffix), (q_hbm, q)))]
    for load in loads:
        load.start()
    tiles = Tiles(reads, prefix, ask, table, asked, packed, got, hot_out, hot_recv,
                  t_send, t_recv, spread_send, spread_recv, local_sem)
    weights = Weights(blocks, w_send, w_recv)
    reduce = Reduce(att, blocks, out, to_right, to_left, at_right, at_left,
                    r_send, r_recv, l_send, l_recv)
    attention = Attention(visible, ids, q, suffix, ka, va, qa, scores, att)

    barrier = pltpu.get_barrier_semaphore()
    for peer in tiles.peers:
        pl.semaphore_signal(barrier, inc=1, device_id=(peer, z), device_id_type=MESH)
    for way in (reduce.right, reduce.left):
        pl.semaphore_signal(barrier, inc=1, device_id=(me, way[4]), device_id_type=MESH)
    tiles.plan()
    loads[0].wait()
    tiles.cut()
    loads[1].wait()
    pl.semaphore_wait(barrier, GROUPS + 1)

    tiles.request()
    tiles.pieces()
    attention.fixed()
    tiles.answer()
    weights.start()
    tiles.spread()
    loads[2].wait()
    loads[3].wait()
    attention.bias(0)
    tiles.receive()
    attention.take(tiles)
    attention.score(0)
    weights.first_axis()
    attention.block(0)
    weights.opposite()
    weights.second_axis(0)
    attention.block(1)
    weights.second_axis(1)
    weights.second_axis(2)
    attention.block(2)
    weights.last(0)
    weights.second_axis(3)
    attention.block(3)
    for jf in range(1, 4):
        weights.last(jf)
    weights.finish()
    for k in (4, 3, 2, 1, 0):
        reduce.stage(k)
    reduce.drain()
    weights.drain()
    tiles.drain()


def layer(reads, visible, prefix, q, suffix, ids, w):
    smem = pl.BlockSpec(memory_space=pltpu.SMEM)
    vmem = pl.BlockSpec(memory_space=pltpu.VMEM)
    hbm = pl.BlockSpec(memory_space=pl.ANY)
    dma = pltpu.SemaphoreType.DMA
    return pl.pallas_call(
        layer_kernel,
        out_shape=jax.ShapeDtypeStruct((TOK, COLS), BF16),
        in_specs=[smem, smem, hbm, hbm, hbm, vmem, hbm],
        out_specs=vmem,
        scratch_shapes=[
            pltpu.VMEM((TPS, TILE, 2 * HEAD), BF16),
            pltpu.VMEM((TOK, HEADS * HEAD), BF16),
            pltpu.VMEM((TOK, 2 * HEAD), BF16),
            dma((4,)),
            pltpu.VMEM((GROUPS, HEADS * HEAD, HEAD), BF16),
            dma((36,)),
            dma((36,)),
            pltpu.VMEM((1, 128), jnp.int32),
            pltpu.VMEM((GROUPS, 1, 128), jnp.int32),
            pltpu.SMEM((GROUPS, 1, 128), jnp.int32),
            pltpu.VMEM((GROUPS - 1, 2 * TILE, HEAD), BF16),
            pltpu.VMEM((GROUPS + 1, 2 * TILE, HEAD), BF16),
            pltpu.VMEM((2 * TILE, HEAD), BF16),
            pltpu.VMEM((GROUPS, 16, HEAD), BF16),
            dma((3,)),
            dma((3,)),
            dma((8,)),
            dma((8,)),
            dma,
            pltpu.VMEM((2, 2 * HEAD, KEYS), BF16),
            pltpu.VMEM((2, KEYS, 2 * HEAD), BF16),
            pltpu.VMEM((2, PAIR, 2 * HEAD), BF16),
            pltpu.VMEM((2, PAIR, KEYS), F32),
            pltpu.VMEM((TOK, HEADS * HEAD), BF16),
            pltpu.VMEM((4, TOK, COLS), BF16),
            pltpu.VMEM((4, TOK, COLS), BF16),
            pltpu.VMEM((4, TOK, COLS), BF16),
            pltpu.VMEM((4, TOK, COLS), BF16),
            dma((4, NBLK)),
            dma((4, NBLK)),
            dma((4, NBLK)),
            dma((4, NBLK)),
        ],
        name="fetch_attend_project_reduce",
        compiler_params=pltpu.CompilerParams(
            collective_id=0, has_side_effects=True, vmem_limit_bytes=52 << 20
        ),
    )(reads, visible, prefix, q, suffix, ids, w)


def local(queries, suffix_kv, prefix_key_value, answer_ids, read_tiles, visible, out_weight):
    return layer(read_tiles, visible, prefix_key_value, queries, suffix_kv, answer_ids,
                 out_weight)


def solution(mesh):
    placed = (
        P("dp", "tensor"),
        P("dp", "tensor"),
        P("dp", None, "tensor"),
        P("dp", None),
        P("dp", None),
        P("dp", None, None),
        P("tensor", "dp"),
    )
    return jax.shard_map(
        local, mesh=mesh, in_specs=placed, out_specs=P("dp", "tensor"), check_vma=False
    )
```

```python
import functools

import jax
import jax.numpy as jnp
from jax import lax
from jax.experimental import pallas as pl
from jax.experimental.pallas import tpu as pltpu
from jax.sharding import PartitionSpec as P

HEAD = 128
TILE = 64
READS = 26
GROUPS = 32
TPS = 8
TOK = 512
HEADS = 8
BLK = 128
NBLK = TOK // BLK
PRE = READS * TILE
KEYS = PRE + 2 * BLK
NZ = 8
COLS = 512
VMEM = 63 << 20
MESH = pl.DeviceIdType.MESH
PAIR = 2 * BLK
BF16 = jnp.bfloat16
F32 = jnp.float32
BIG = -1e30
LOG2E = 1.4426950408889634
SCALE = HEAD ** (-0.5) * LOG2E


def coords():
    g = lax.axis_index("dp")
    return g // 8, lax.rem(g // 2, 4), lax.rem(g, 2), lax.axis_index("tensor")


def place(x, y, c):
    return lax.rem(x, 4) * 8 + lax.rem(y, 4) * 2 + lax.rem(c, 2)


def remote(src, dst, send, recv, dp, tensor):
    return pltpu.make_async_remote_copy(
        src_ref=src, dst_ref=dst, send_sem=send, recv_sem=recv,
        device_id=(dp, tensor), device_id_type=MESH,
    )


class Tiles:
    def __init__(self, reads, prefix, ask, table, asked, packed, got, hot_out, hot_recv,
                 sem_send, sem_recv, spread_send, spread_recv, local_sem):
        self.reads, self.prefix, self.ask, self.table, self.asked = reads, prefix, ask, table, asked
        self.packed, self.got, self.hot_out, self.hot_recv = packed, got, hot_out, hot_recv
        self.sem_send, self.sem_recv, self.local_sem = sem_send, sem_recv, local_sem
        self.spread_send, self.spread_recv = spread_send, spread_recv
        self.x, self.y, self.c, self.z = coords()
        self.me = lax.axis_index("dp")
        self.peers = [place(self.x + k // 8, self.y + (k // 2) % 4, self.c + k % 2)
                      for k in range(1, GROUPS)]

    def plan(self):
        lane = lax.broadcasted_iota(jnp.int32, (1, 128), 1)
        first = jnp.full((1, 128), TPS, jnp.int32)
        last = jnp.full((1, 128), -1, jnp.int32)
        self.tiles = [self.reads[0, r] for r in range(READS)]
        for tile in self.tiles:
            here = lane == tile // TPS
            first = jnp.where(here, jnp.minimum(first, tile % TPS), first)
            last = jnp.where(here, jnp.maximum(last, tile % TPS), last)
        twice = last > first
        self.hot_owner = jnp.max(jnp.where(twice, lane, 0))
        self.hot_second = jnp.max(jnp.where(twice, last, 0))
        mine = jnp.where(first == TPS, 0, first)
        self.ask[...] = mine
        self.table[pl.ds(self.me, 1)] = mine[None]

    def cut(self):
        second = self.prefix[self.hot_second]
        self.hot_out[pl.ds(0, TILE)] = second[:, :HEAD]
        self.hot_out[pl.ds(TILE, TILE)] = second[:, HEAD:]
        self.part = pl.multiple_of(lax.rem(self.me, 8) * 16, 16)
        self.hot_recv[pl.ds(self.me, 1)] = self.hot_out[pl.ds(self.part, 16)][None]

    def request(self):
        for peer in self.peers:
            remote(self.ask, self.table.at[self.me], self.sem_send.at[0], self.sem_recv.at[0],
                   peer, self.z).start()

    def pieces(self):
        for peer in self.peers:
            part = pl.multiple_of(lax.rem(peer, 8) * 16, 16)
            remote(self.hot_out.at[pl.ds(part, 16)], self.hot_recv.at[self.me],
                   self.sem_send.at[1], self.sem_recv.at[1], peer, self.z).start()

    def wait_all(self, ref, sem):
        part = ref.at[pl.ds(0, GROUPS - 1)]
        pltpu.make_async_copy(part, part, sem).wait()

    def answer(self):
        me, z = self.me, self.z
        self.wait_all(self.table, self.sem_recv.at[0])
        load = pltpu.make_async_copy(self.table, self.asked, self.local_sem)
        load.start()
        load.wait()
        for k, peer in enumerate(self.peers):
            tile = self.prefix[self.asked[peer, 0, me]]
            self.packed[k, pl.ds(0, TILE)] = tile[:, :HEAD]
            self.packed[k, pl.ds(TILE, TILE)] = tile[:, HEAD:]
            remote(self.packed.at[k], self.got.at[me], self.sem_send.at[2],
                   self.sem_recv.at[2], peer, z).start()
        own = self.prefix[self.asked[me, 0, me]]
        self.got[pl.ds(me, 1), pl.ds(0, TILE)] = own[:, :HEAD][None]
        self.got[pl.ds(me, 1), pl.ds(TILE, TILE)] = own[:, HEAD:][None]

    def spread(self):
        self.wait_all(self.hot_recv, self.sem_recv.at[1])
        ref = self.got.at[GROUPS, pl.ds(self.part, 16)]
        self.got[GROUPS, pl.ds(self.part, 16)] = self.hot_recv[self.hot_owner]
        self.spreads = []
        for k in range(1, 8):
            copy = remote(ref, ref, self.spread_send.at[k], self.spread_recv.at[k],
                          place(self.x, self.y + k // 2, self.c + k % 2), self.z)
            copy.start()
            self.spreads.append(copy)

    def receive(self):
        self.wait_all(self.got, self.sem_recv.at[2])
        for copy in self.spreads:
            copy.wait_recv()

    def tile(self, r):
        owner = self.tiles[r] // TPS
        second = (owner == self.hot_owner) & (self.tiles[r] % TPS == self.hot_second)
        return self.got[jnp.where(second, GROUPS, owner)]

    def drain(self):
        self.wait_all(self.table, self.sem_send.at[0])
        self.wait_all(self.hot_recv, self.sem_send.at[1])
        self.wait_all(self.packed, self.sem_send.at[2])
        for copy in self.spreads:
            copy.wait_send()


class Weights:
    def __init__(self, blocks, send, recv):
        self.blocks, self.send, self.recv = blocks, send, recv
        self.x, self.y, self.c, self.z = coords()
        c = self.c
        x_mate, y_mate = 1 + 2 * lax.rem(self.x, 2), 1 + 2 * lax.rem(self.y, 2)
        first = x_mate * (1 - c) + y_mate * c
        second = y_mate * (1 - c) + x_mate * c
        self.f, self.s = (0, first, 4 - first, 2), (0, second, 4 - second, 2)
        self.sibling = place(self.x, self.y, c + 1)

    def at(self, jf, js):
        c = self.c
        f, s = self.f[jf], self.s[js]
        return place(self.x + f * (1 - c) + s * c, self.y + s * (1 - c) + f * c, c)

    def other_core(self, jf, js):
        c = 1 - self.c
        f, s = self.s[jf], self.f[js]
        return place(self.x + f * (1 - c) + s * c, self.y + s * (1 - c) + f * c, c)

    def copy(self, kind, block, dp, rows=None):
        ref = self.blocks.at[block]
        if rows is not None:
            ref = ref.at[pl.ds(rows * 512, 512)]
        return remote(ref, ref, self.send.at[kind], self.recv.at[kind], dp, self.z)

    def sent(self, kind):
        if kind < 2:
            return self.copy(kind, self.at(0, 0), self.at(kind + 1, 0))
        if kind < 4:
            return self.copy(kind, self.at(kind - 1, 0), self.at(4 - kind, 0), rows=kind - 2)
        if kind < 12:
            j, way = (kind - 4) // 2, kind % 2
            return self.copy(kind, self.at(j, 0), self.at(0, 1 + way))
        if kind < 20:
            j, way = (kind - 12) // 2, kind % 2
            return self.copy(kind, self.at(j, 1 + way), self.at(0, 2 - way), rows=way)
        return self.copy(kind, self.at((kind - 20) // 4, kind % 4), self.sibling)

    def go(self, *kinds):
        for kind in kinds:
            self.sent(kind).start()

    def come(self, *kinds):
        me = self.at(0, 0)
        for kind in kinds:
            if kind < 2:
                copy = self.copy(kind, self.at(kind + 1, 0), me)
            elif kind < 4:
                copy = self.copy(kind, self.at(3, 0), me, rows=kind - 2)
            elif kind < 12:
                copy = self.copy(kind, self.at((kind - 4) // 2, 1 + kind % 2), me)
            elif kind < 20:
                copy = self.copy(kind, self.at((kind - 12) // 2, 3), me, rows=kind % 2)
            else:
                copy = self.copy(kind, self.other_core((kind - 20) // 4, kind % 4), me)
            copy.wait_recv()

    def start(self):
        self.go(0, 1, 4, 5, 20)

    def ring(self):
        self.come(0)
        self.go(2, 6, 7, 24)
        self.come(1)
        self.go(3, 8, 9, 28)

    def opposite(self):
        self.come(2, 3)
        self.go(10, 11, 32)

    def across(self, j):
        self.come(4 + 2 * j, 5 + 2 * j)
        self.go(12 + 2 * j, 13 + 2 * j, 21 + 4 * j, 22 + 4 * j)

    def last(self, j):
        self.come(12 + 2 * j, 13 + 2 * j)
        self.go(23 + 4 * j)

    def finish(self):
        self.come(*range(20, 36))

    def drain(self):
        for kind in range(36):
            self.sent(kind).wait_send()


class Reduce:
    def __init__(self, att, blocks, out, to_right, to_left, at_right, at_left,
                 r_send, r_recv, l_send, l_recv):
        self.att, self.blocks, self.out = att, blocks, out
        self.me, self.z = lax.axis_index("dp"), lax.axis_index("tensor")
        right, left = lax.rem(self.z + 1, NZ), lax.rem(self.z + NZ - 1, NZ)
        self.right = (to_right, at_right, r_send, r_recv, right)
        self.left = (to_left, at_left, l_send, l_recv, left)

    def rows(self, b):
        return pl.ds(pl.multiple_of(b * BLK, BLK), BLK)

    def project(self, b, hops):
        base = lax.rem(self.z + NZ + hops, NZ) * 4
        wide = jnp.concatenate([self.blocks[base + i] for i in range(4)], axis=1)
        return jnp.dot(self.att[self.rows(b), :], wide, preferred_element_type=F32)

    def copy(self, way, k, b):
        to, at, send, recv, peer = way
        part = (k - 1, self.rows(b), pl.ds(0, COLS // 2 if k == 4 else COLS))
        return remote(to.at[part], at.at[part], send.at[k - 1, b], recv.at[k - 1, b],
                      self.me, peer)

    def send(self, way, k, b, value):
        way[0][k - 1, self.rows(b), pl.ds(0, value.shape[1])] = value.astype(BF16)
        self.copy(way, k, b).start()

    def arrived(self, way, k, b):
        self.copy(way, k + 1, b).wait_recv()
        return way[1][k, self.rows(b), pl.ds(0, COLS // 2 if k == 3 else COLS)].astype(F32)

    def stage(self, k):
        half = COLS // 2

        def body(b, _):
            if k == 4:
                part = self.project(b, 4)
                self.send(self.right, 4, b, part[:, :half])
                self.send(self.left, 4, b, part[:, half:])
            elif k == 0:
                part = self.project(b, 0)
                part = part + self.arrived(self.right, 0, b)
                part = part + self.arrived(self.left, 0, b)
                self.out[self.rows(b), :] = part.astype(BF16)
            else:
                for way, hops in ((self.right, k), (self.left, -k)):
                    part = self.project(b, hops)
                    come = self.arrived(way, k, b)
                    if k == 3 and hops > 0:
                        part = jnp.concatenate([part[:, :half] + come, part[:, half:]], axis=1)
                    elif k == 3:
                        part = jnp.concatenate([part[:, :half], part[:, half:] + come], axis=1)
                    else:
                        part = part + come
                    self.send(way, k, b, part)
            return 0

        lax.fori_loop(0, NBLK, body, 0)

    def drain(self):
        def body(b, _):
            for k in range(1, 5):
                self.copy(self.right, k, b).wait_send()
                self.copy(self.left, k, b).wait_send()
            return 0

        lax.fori_loop(0, NBLK, body, 0)


class Attention:
    def __init__(self, visible, ids, q, suffix, ka, va, qa, scores, att):
        self.visible, self.ids, self.q, self.suffix = visible, ids, q, suffix
        self.ka, self.va, self.qa, self.scores, self.att = ka, va, qa, scores, att

    def fixed(self):
        row = lax.broadcasted_iota(jnp.int32, (BLK, BLK), 0)
        col = lax.broadcasted_iota(jnp.int32, (BLK, BLK), 1)
        self.row, self.col = row, col
        eye = jnp.where(row == col, 1.0, 0.0).astype(BF16)
        for slot in range(2):
            for j in range(2):
                self.qa[slot, pl.ds(j * BLK, BLK), pl.ds(HEAD, HEAD)] = eye
            self.va[slot, :, pl.ds(HEAD, HEAD)] = jnp.ones((KEYS, HEAD), BF16)
        self.down = [jnp.broadcast_to(self.ids[:, pl.ds(b * BLK, BLK)].astype(F32), (BLK, BLK)).T
                     for b in range(NBLK)]

    def bias(self, b):
        slot = b % 2
        second = self.down[b] >= 8.0
        for r in range(0, READS, 2):
            lines = [jnp.where(self.col < TILE,
                               jnp.where(self.visible[0, n, r] > 0, 0.0, BIG),
                               jnp.where(self.visible[0, n, r + 1] > 0, 0.0, BIG))
                     for n in range(2)]
            self.ka[slot, pl.ds(HEAD, HEAD), pl.ds(r * TILE, BLK)] = jnp.where(
                second, lines[1], lines[0]).astype(BF16)
        start = max(b - 1, 0) * BLK
        for part in range(2):
            base = start + part * BLK
            at = pl.ds(PRE + part * BLK, BLK)
            same = self.down[b] == self.ids[:, pl.ds(base, BLK)].astype(F32)
            seen = same & (self.col + base <= self.row + b * BLK)
            self.ka[slot, pl.ds(HEAD, HEAD), at] = jnp.where(seen, 0.0, BIG).astype(BF16)
            self.ka[slot, pl.ds(0, HEAD), at] = self.suffix[pl.ds(base, BLK), pl.ds(0, HEAD)].T
            self.va[slot, at, pl.ds(0, HEAD)] = self.suffix[pl.ds(base, BLK), pl.ds(HEAD, HEAD)]

    def take(self, tiles):
        for r in range(0, READS, 2):
            one, two = tiles.tile(r), tiles.tile(r + 1)
            across = jnp.concatenate([one[:TILE], two[:TILE]], axis=0).T
            for slot in range(2):
                self.ka[slot, pl.ds(0, HEAD), pl.ds(r * TILE, BLK)] = across
                self.va[slot, pl.ds(r * TILE, TILE), pl.ds(0, HEAD)] = one[TILE:]
                self.va[slot, pl.ds((r + 1) * TILE, TILE), pl.ds(0, HEAD)] = two[TILE:]

    def score(self, i):
        b, h = i // 4, i % 4 * 2
        for j in range(2):
            self.qa[i % 2, pl.ds(j * BLK, BLK), pl.ds(0, HEAD)] = (
                self.q[pl.ds(b * BLK, BLK), pl.ds((h + j) * HEAD, HEAD)])
        self.scores[i % 2] = jnp.dot(self.qa[i % 2], self.ka[b % 2], preferred_element_type=F32)

    def rest(self, i):
        b, h = i // 4, i % 4 * 2
        scores = self.scores[i % 2]
        top = jnp.max(scores, axis=1, keepdims=True)
        probs = jnp.exp2((scores - top) * SCALE).astype(BF16)
        mixed = jnp.dot(probs, self.va[b % 2], preferred_element_type=F32)
        done = (mixed[:, :HEAD] / mixed[:, HEAD:]).astype(BF16)
        for j in range(2):
            self.att[pl.ds(b * BLK, BLK), pl.ds((h + j) * HEAD, HEAD)] = done[j * BLK:(j + 1) * BLK]

    def pair(self, i):
        if i % 4 == 3 and i + 1 < 4 * NBLK:
            self.bias(i // 4 + 1)
        if i + 1 < 4 * NBLK:
            self.score(i + 1)
        self.rest(i)


def layer_kernel(reads, visible, prefix_hbm, q_hbm, suffix_hbm, ids, w_hbm, out,
                 prefix, q, suffix, load_sem, blocks, w_send, w_recv,
                 ask, table, asked, packed, got, hot_out, hot_recv,
                 t_send, t_recv, spread_send, spread_recv, local_sem,
                 ka, va, qa, scores, att,
                 to_right, to_left, at_right, at_left, r_send, r_recv, l_send, l_recv):
    me, z = lax.axis_index("dp"), lax.axis_index("tensor")
    loads = [pltpu.make_async_copy(src, dst, load_sem.at[i]) for i, (src, dst) in enumerate(
        ((prefix_hbm, prefix), (w_hbm, blocks.at[me]), (suffix_hbm, suffix), (q_hbm, q)))]
    for load in loads:
        load.start()
    tiles = Tiles(reads, prefix, ask, table, asked, packed, got, hot_out, hot_recv,
                  t_send, t_recv, spread_send, spread_recv, local_sem)
    weights = Weights(blocks, w_send, w_recv)
    reduce = Reduce(att, blocks, out, to_right, to_left, at_right, at_left,
                    r_send, r_recv, l_send, l_recv)
    attention = Attention(visible, ids, q, suffix, ka, va, qa, scores, att)

    barrier = pltpu.get_barrier_semaphore()
    for peer in tiles.peers:
        pl.semaphore_signal(barrier, inc=1, device_id=(peer, z), device_id_type=MESH)
    for way in (reduce.right, reduce.left):
        pl.semaphore_signal(barrier, inc=1, device_id=(me, way[4]), device_id_type=MESH)
    tiles.plan()
    loads[0].wait()
    tiles.cut()
    loads[1].wait()
    pl.semaphore_wait(barrier, GROUPS + 1)

    tiles.request()
    weights.start()
    tiles.pieces()
    attention.fixed()
    tiles.answer()
    weights.ring()
    tiles.spread()
    loads[2].wait()
    loads[3].wait()
    attention.bias(0)
    weights.opposite()
    weights.across(0)
    tiles.receive()
    attention.take(tiles)
    attention.score(0)
    beside = {
        0: [(weights.across, 1)], 2: [(weights.across, 2)], 4: [(weights.across, 3)],
        6: [(weights.last, 0)], 8: [(weights.last, 1)], 10: [(weights.last, 2)],
        12: [(weights.last, 3)],
    }
    for i in range(4 * NBLK):
        attention.pair(i)
        for step, *j in beside.get(i, ()):
            step(*j)
    weights.finish()
    for k in (4, 3, 2, 1, 0):
        reduce.stage(k)
    reduce.drain()
    weights.drain()
    tiles.drain()


def layer(reads, visible, prefix, q, suffix, ids, w):
    smem = pl.BlockSpec(memory_space=pltpu.SMEM)
    vmem = pl.BlockSpec(memory_space=pltpu.VMEM)
    hbm = pl.BlockSpec(memory_space=pl.ANY)
    dma = pltpu.SemaphoreType.DMA
    return pl.pallas_call(
        layer_kernel,
        out_shape=jax.ShapeDtypeStruct((TOK, COLS), BF16),
        in_specs=[smem, smem, hbm, hbm, hbm, vmem, hbm],
        out_specs=vmem,
        scratch_shapes=[
            pltpu.VMEM((TPS, TILE, 2 * HEAD), BF16),
            pltpu.VMEM((TOK, HEADS * HEAD), BF16),
            pltpu.VMEM((TOK, 2 * HEAD), BF16),
            dma((4,)),
            pltpu.VMEM((GROUPS, HEADS * HEAD, HEAD), BF16),
            dma((36,)),
            dma((36,)),
            pltpu.VMEM((1, 128), jnp.int32),
            pltpu.VMEM((GROUPS, 1, 128), jnp.int32),
            pltpu.SMEM((GROUPS, 1, 128), jnp.int32),
            pltpu.VMEM((GROUPS - 1, 2 * TILE, HEAD), BF16),
            pltpu.VMEM((GROUPS + 1, 2 * TILE, HEAD), BF16),
            pltpu.VMEM((2 * TILE, HEAD), BF16),
            pltpu.VMEM((GROUPS, 16, HEAD), BF16),
            dma((3,)),
            dma((3,)),
            dma((8,)),
            dma((8,)),
            dma,
            pltpu.VMEM((2, 2 * HEAD, KEYS), BF16),
            pltpu.VMEM((2, KEYS, 2 * HEAD), BF16),
            pltpu.VMEM((2, PAIR, 2 * HEAD), BF16),
            pltpu.VMEM((2, PAIR, KEYS), F32),
            pltpu.VMEM((TOK, HEADS * HEAD), BF16),
            pltpu.VMEM((4, TOK, COLS), BF16),
            pltpu.VMEM((4, TOK, COLS), BF16),
            pltpu.VMEM((4, TOK, COLS), BF16),
            pltpu.VMEM((4, TOK, COLS), BF16),
            dma((4, NBLK)),
            dma((4, NBLK)),
            dma((4, NBLK)),
            dma((4, NBLK)),
        ],
        name="fetch_attend_project_reduce",
        compiler_params=pltpu.CompilerParams(
            collective_id=0, has_side_effects=True, vmem_limit_bytes=VMEM
        ),
    )(reads, visible, prefix, q, suffix, ids, w)


def local(queries, suffix_kv, prefix_key_value, answer_ids, read_tiles, visible, out_weight):
    return layer(read_tiles, visible, prefix_key_value, queries, suffix_kv, answer_ids,
                 out_weight)


def solution(mesh):
    placed = (
        P("dp", "tensor"),
        P("dp", "tensor"),
        P("dp", None, "tensor"),
        P("dp", None),
        P("dp", None),
        P("dp", None, None),
        P("tensor", "dp"),
    )
    return jax.shard_map(
        local, mesh=mesh, in_specs=placed, out_specs=P("dp", "tensor"), check_vma=False
    )
```

```python
import functools

import jax
import jax.numpy as jnp
from jax import lax
from jax.experimental import pallas as pl
from jax.experimental.pallas import tpu as pltpu
from jax.sharding import PartitionSpec as P

HEAD = 128
TILE = 64
READS = 26
GROUPS = 32
TPS = 8
TOK = 512
HEADS = 8
BLK = 128
NBLK = TOK // BLK
PRE = READS * TILE
KEYS = PRE + 2 * BLK
NZ = 8
COLS = 512
VMEM = 63 << 20
MESH = pl.DeviceIdType.MESH
PAIR = 2 * BLK
BF16 = jnp.bfloat16
F32 = jnp.float32
BIG = -1e30
LOG2E = 1.4426950408889634
SCALE = HEAD ** (-0.5) * LOG2E


def coords():
    g = lax.axis_index("dp")
    return g // 8, lax.rem(g // 2, 4), lax.rem(g, 2), lax.axis_index("tensor")


def place(x, y, c):
    return lax.rem(x, 4) * 8 + lax.rem(y, 4) * 2 + lax.rem(c, 2)


def remote(src, dst, send, recv, dp, tensor):
    return pltpu.make_async_remote_copy(
        src_ref=src, dst_ref=dst, send_sem=send, recv_sem=recv,
        device_id=(dp, tensor), device_id_type=MESH,
    )


class Tiles:
    def __init__(self, reads, prefix, ask, table, asked, packed, got, hot_out, hot_recv,
                 sem_send, sem_recv, spread_send, spread_recv, local_sem):
        self.reads, self.prefix, self.ask, self.table, self.asked = reads, prefix, ask, table, asked
        self.packed, self.got, self.hot_out, self.hot_recv = packed, got, hot_out, hot_recv
        self.sem_send, self.sem_recv, self.local_sem = sem_send, sem_recv, local_sem
        self.spread_send, self.spread_recv = spread_send, spread_recv
        self.x, self.y, self.c, self.z = coords()
        self.me = lax.axis_index("dp")
        self.peers = [place(self.x + k // 8, self.y + (k // 2) % 4, self.c + k % 2)
                      for k in range(1, GROUPS)]

    def plan(self):
        lane = lax.broadcasted_iota(jnp.int32, (1, 128), 1)
        first = jnp.full((1, 128), TPS, jnp.int32)
        last = jnp.full((1, 128), -1, jnp.int32)
        self.tiles = [self.reads[0, r] for r in range(READS)]
        for tile in self.tiles:
            here = lane == tile // TPS
            first = jnp.where(here, jnp.minimum(first, tile % TPS), first)
            last = jnp.where(here, jnp.maximum(last, tile % TPS), last)
        twice = last > first
        self.hot_owner = jnp.max(jnp.where(twice, lane, 0))
        self.hot_second = jnp.max(jnp.where(twice, last, 0))
        mine = jnp.where(first == TPS, 0, first)
        self.ask[...] = mine
        self.table[pl.ds(self.me, 1)] = mine[None]

    def cut(self):
        second = self.prefix[self.hot_second]
        self.hot_out[pl.ds(0, TILE)] = second[:, :HEAD]
        self.hot_out[pl.ds(TILE, TILE)] = second[:, HEAD:]
        self.part = pl.multiple_of(lax.rem(self.me, 8) * 16, 16)
        self.hot_recv[pl.ds(self.me, 1)] = self.hot_out[pl.ds(self.part, 16)][None]

    def request(self):
        for peer in self.peers:
            remote(self.ask, self.table.at[self.me], self.sem_send.at[0], self.sem_recv.at[0],
                   peer, self.z).start()

    def pieces(self):
        for peer in self.peers:
            part = pl.multiple_of(lax.rem(peer, 8) * 16, 16)
            remote(self.hot_out.at[pl.ds(part, 16)], self.hot_recv.at[self.me],
                   self.sem_send.at[1], self.sem_recv.at[1], peer, self.z).start()

    def wait_all(self, ref, sem):
        part = ref.at[pl.ds(0, GROUPS - 1)]
        pltpu.make_async_copy(part, part, sem).wait()

    def answer(self):
        me, z = self.me, self.z
        self.wait_all(self.table, self.sem_recv.at[0])
        load = pltpu.make_async_copy(self.table, self.asked, self.local_sem)
        load.start()
        load.wait()
        for k, peer in enumerate(self.peers):
            tile = self.prefix[self.asked[peer, 0, me]]
            self.packed[k, pl.ds(0, TILE)] = tile[:, :HEAD]
            self.packed[k, pl.ds(TILE, TILE)] = tile[:, HEAD:]
            remote(self.packed.at[k], self.got.at[me], self.sem_send.at[2],
                   self.sem_recv.at[2], peer, z).start()
        own = self.prefix[self.asked[me, 0, me]]
        self.got[pl.ds(me, 1), pl.ds(0, TILE)] = own[:, :HEAD][None]
        self.got[pl.ds(me, 1), pl.ds(TILE, TILE)] = own[:, HEAD:][None]

    def spread(self):
        self.wait_all(self.hot_recv, self.sem_recv.at[1])
        ref = self.got.at[GROUPS, pl.ds(self.part, 16)]
        self.got[GROUPS, pl.ds(self.part, 16)] = self.hot_recv[self.hot_owner]
        self.spreads = []
        for k in range(1, 8):
            copy = remote(ref, ref, self.spread_send.at[k], self.spread_recv.at[k],
                          place(self.x, self.y + k // 2, self.c + k % 2), self.z)
            copy.start()
            self.spreads.append(copy)

    def receive(self):
        self.wait_all(self.got, self.sem_recv.at[2])
        for copy in self.spreads:
            copy.wait_recv()

    def tile(self, r):
        owner = self.tiles[r] // TPS
        second = (owner == self.hot_owner) & (self.tiles[r] % TPS == self.hot_second)
        return self.got[jnp.where(second, GROUPS, owner)]

    def drain(self):
        self.wait_all(self.table, self.sem_send.at[0])
        self.wait_all(self.hot_recv, self.sem_send.at[1])
        self.wait_all(self.packed, self.sem_send.at[2])
        for copy in self.spreads:
            copy.wait_send()


class Weights:
    def __init__(self, blocks, send, recv):
        self.blocks, self.send, self.recv = blocks, send, recv
        self.x, self.y, self.c, self.z = coords()
        c = self.c
        x_mate, y_mate = 1 + 2 * lax.rem(self.x, 2), 1 + 2 * lax.rem(self.y, 2)
        first = x_mate * (1 - c) + y_mate * c
        second = y_mate * (1 - c) + x_mate * c
        self.f, self.s = (0, first, 4 - first, 2), (0, second, 4 - second, 2)
        self.sibling = place(self.x, self.y, c + 1)

    def at(self, jf, js):
        c = self.c
        f, s = self.f[jf], self.s[js]
        return place(self.x + f * (1 - c) + s * c, self.y + s * (1 - c) + f * c, c)

    def other_core(self, jf, js):
        c = 1 - self.c
        f, s = self.s[jf], self.f[js]
        return place(self.x + f * (1 - c) + s * c, self.y + s * (1 - c) + f * c, c)

    def copy(self, kind, block, dp, rows=None):
        ref = self.blocks.at[block]
        if rows is not None:
            ref = ref.at[pl.ds(rows * 512, 512)]
        return remote(ref, ref, self.send.at[kind], self.recv.at[kind], dp, self.z)

    def sent(self, kind):
        if kind < 2:
            return self.copy(kind, self.at(0, 0), self.at(kind + 1, 0))
        if kind < 4:
            return self.copy(kind, self.at(kind - 1, 0), self.at(4 - kind, 0), rows=kind - 2)
        if kind < 12:
            j, way = (kind - 4) // 2, kind % 2
            return self.copy(kind, self.at(j, 0), self.at(0, 1 + way))
        if kind < 20:
            j, way = (kind - 12) // 2, kind % 2
            return self.copy(kind, self.at(j, 1 + way), self.at(0, 2 - way), rows=way)
        return self.copy(kind, self.at((kind - 20) // 4, kind % 4), self.sibling)

    def go(self, *kinds):
        for kind in kinds:
            self.sent(kind).start()

    def come(self, *kinds):
        me = self.at(0, 0)
        for kind in kinds:
            if kind < 2:
                copy = self.copy(kind, self.at(kind + 1, 0), me)
            elif kind < 4:
                copy = self.copy(kind, self.at(3, 0), me, rows=kind - 2)
            elif kind < 12:
                copy = self.copy(kind, self.at((kind - 4) // 2, 1 + kind % 2), me)
            elif kind < 20:
                copy = self.copy(kind, self.at((kind - 12) // 2, 3), me, rows=kind % 2)
            else:
                copy = self.copy(kind, self.other_core((kind - 20) // 4, kind % 4), me)
            copy.wait_recv()

    def start(self):
        self.go(0, 1, 4, 5, 20)

    def ring(self):
        self.come(0)
        self.go(2, 6, 7, 24)
        self.come(1)
        self.go(3, 8, 9, 28)

    def opposite(self):
        self.come(2, 3)
        self.go(10, 11, 32)

    def across(self, j):
        self.come(4 + 2 * j, 5 + 2 * j)
        self.go(12 + 2 * j, 13 + 2 * j, 21 + 4 * j, 22 + 4 * j)

    def last(self, j):
        self.come(12 + 2 * j, 13 + 2 * j)
        self.go(23 + 4 * j)

    def finish(self):
        self.come(*range(20, 36))

    def drain(self):
        for kind in range(36):
            self.sent(kind).wait_send()


class Reduce:
    def __init__(self, att, blocks, out, to_right, to_left, at_right, at_left,
                 r_send, r_recv, l_send, l_recv):
        self.att, self.blocks, self.out = att, blocks, out
        self.me, self.z = lax.axis_index("dp"), lax.axis_index("tensor")
        right, left = lax.rem(self.z + 1, NZ), lax.rem(self.z + NZ - 1, NZ)
        self.right = (to_right, at_right, r_send, r_recv, right)
        self.left = (to_left, at_left, l_send, l_recv, left)

    def rows(self, b):
        return pl.ds(pl.multiple_of(b * BLK, BLK), BLK)

    def project(self, b, hops):
        base = lax.rem(self.z + NZ + hops, NZ) * 4
        wide = jnp.concatenate([self.blocks[base + i] for i in range(4)], axis=1)
        return jnp.dot(self.att[self.rows(b), :], wide, preferred_element_type=F32)

    def copy(self, way, k, b):
        to, at, send, recv, peer = way
        part = (k - 1, self.rows(b), pl.ds(0, COLS // 2 if k == 4 else COLS))
        return remote(to.at[part], at.at[part], send.at[k - 1, b], recv.at[k - 1, b],
                      self.me, peer)

    def send(self, way, k, b, value):
        way[0][k - 1, self.rows(b), pl.ds(0, value.shape[1])] = value.astype(BF16)
        self.copy(way, k, b).start()

    def arrived(self, way, k, b):
        self.copy(way, k + 1, b).wait_recv()
        return way[1][k, self.rows(b), pl.ds(0, COLS // 2 if k == 3 else COLS)].astype(F32)

    def stage(self, k, first=0, end=NBLK):
        half = COLS // 2

        def body(b, _):
            if k == 4:
                part = self.project(b, 4)
                self.send(self.right, 4, b, part[:, :half])
                self.send(self.left, 4, b, part[:, half:])
            elif k == 0:
                part = self.project(b, 0)
                part = part + self.arrived(self.right, 0, b)
                part = part + self.arrived(self.left, 0, b)
                self.out[self.rows(b), :] = part.astype(BF16)
            else:
                for way, hops in ((self.right, k), (self.left, -k)):
                    part = self.project(b, hops)
                    come = self.arrived(way, k, b)
                    if k == 3 and hops > 0:
                        part = jnp.concatenate([part[:, :half] + come, part[:, half:]], axis=1)
                    elif k == 3:
                        part = jnp.concatenate([part[:, :half], part[:, half:] + come], axis=1)
                    else:
                        part = part + come
                    self.send(way, k, b, part)
            return 0

        lax.fori_loop(first, end, body, 0)

    def drain(self):
        def body(b, _):
            for k in range(1, 5):
                self.copy(self.right, k, b).wait_send()
                self.copy(self.left, k, b).wait_send()
            return 0

        lax.fori_loop(0, NBLK, body, 0)


class Attention:
    def __init__(self, visible, ids, q, suffix, ka, va, qa, scores, att):
        self.visible, self.ids, self.q, self.suffix = visible, ids, q, suffix
        self.ka, self.va, self.qa, self.scores, self.att = ka, va, qa, scores, att

    def fixed(self):
        row = lax.broadcasted_iota(jnp.int32, (BLK, BLK), 0)
        col = lax.broadcasted_iota(jnp.int32, (BLK, BLK), 1)
        self.row, self.col = row, col
        eye = jnp.where(row == col, 1.0, 0.0).astype(BF16)
        for slot in range(2):
            for j in range(2):
                self.qa[slot, pl.ds(j * BLK, BLK), pl.ds(HEAD, HEAD)] = eye
            self.va[slot, :, pl.ds(HEAD, HEAD)] = jnp.ones((KEYS, HEAD), BF16)
        self.down = [jnp.broadcast_to(self.ids[:, pl.ds(b * BLK, BLK)].astype(F32), (BLK, BLK)).T
                     for b in range(NBLK)]

    def bias(self, b):
        slot = b % 2
        second = self.down[b] >= 8.0
        for r in range(0, READS, 2):
            lines = [jnp.where(self.col < TILE,
                               jnp.where(self.visible[0, n, r] > 0, 0.0, BIG),
                               jnp.where(self.visible[0, n, r + 1] > 0, 0.0, BIG))
                     for n in range(2)]
            self.ka[slot, pl.ds(HEAD, HEAD), pl.ds(r * TILE, BLK)] = jnp.where(
                second, lines[1], lines[0]).astype(BF16)
        start = max(b - 1, 0) * BLK
        for part in range(2):
            base = start + part * BLK
            at = pl.ds(PRE + part * BLK, BLK)
            same = self.down[b] == self.ids[:, pl.ds(base, BLK)].astype(F32)
            seen = same & (self.col + base <= self.row + b * BLK)
            self.ka[slot, pl.ds(HEAD, HEAD), at] = jnp.where(seen, 0.0, BIG).astype(BF16)
            self.ka[slot, pl.ds(0, HEAD), at] = self.suffix[pl.ds(base, BLK), pl.ds(0, HEAD)].T
            self.va[slot, at, pl.ds(0, HEAD)] = self.suffix[pl.ds(base, BLK), pl.ds(HEAD, HEAD)]

    def take(self, tiles):
        for r in range(0, READS, 2):
            one, two = tiles.tile(r), tiles.tile(r + 1)
            across = jnp.concatenate([one[:TILE], two[:TILE]], axis=0).T
            for slot in range(2):
                self.ka[slot, pl.ds(0, HEAD), pl.ds(r * TILE, BLK)] = across
                self.va[slot, pl.ds(r * TILE, TILE), pl.ds(0, HEAD)] = one[TILE:]
                self.va[slot, pl.ds((r + 1) * TILE, TILE), pl.ds(0, HEAD)] = two[TILE:]

    def score(self, i):
        b, h = i // 4, i % 4 * 2
        for j in range(2):
            self.qa[i % 2, pl.ds(j * BLK, BLK), pl.ds(0, HEAD)] = (
                self.q[pl.ds(b * BLK, BLK), pl.ds((h + j) * HEAD, HEAD)])
        self.scores[i % 2] = jnp.dot(self.qa[i % 2], self.ka[b % 2], preferred_element_type=F32)

    def rest(self, i):
        b, h = i // 4, i % 4 * 2
        scores = self.scores[i % 2]
        top = jnp.max(scores, axis=1, keepdims=True)
        probs = jnp.exp2((scores - top) * SCALE).astype(BF16)
        mixed = jnp.dot(probs, self.va[b % 2], preferred_element_type=F32)
        done = (mixed[:, :HEAD] / mixed[:, HEAD:]).astype(BF16)
        for j in range(2):
            self.att[pl.ds(b * BLK, BLK), pl.ds((h + j) * HEAD, HEAD)] = done[j * BLK:(j + 1) * BLK]

    def pair(self, i):
        if i % 4 == 3 and i + 1 < 4 * NBLK:
            self.bias(i // 4 + 1)
        if i + 1 < 4 * NBLK:
            self.score(i + 1)
        self.rest(i)


def layer_kernel(reads, visible, prefix_hbm, q_hbm, suffix_hbm, ids, w_hbm, out,
                 prefix, q, suffix, load_sem, blocks, w_send, w_recv,
                 ask, table, asked, packed, got, hot_out, hot_recv,
                 t_send, t_recv, spread_send, spread_recv, local_sem,
                 ka, va, qa, scores, att,
                 to_right, to_left, at_right, at_left, r_send, r_recv, l_send, l_recv):
    me, z = lax.axis_index("dp"), lax.axis_index("tensor")
    loads = [pltpu.make_async_copy(src, dst, load_sem.at[i]) for i, (src, dst) in enumerate(
        ((prefix_hbm, prefix), (w_hbm, blocks.at[me]), (suffix_hbm, suffix), (q_hbm, q)))]
    for load in loads:
        load.start()
    tiles = Tiles(reads, prefix, ask, table, asked, packed, got, hot_out, hot_recv,
                  t_send, t_recv, spread_send, spread_recv, local_sem)
    weights = Weights(blocks, w_send, w_recv)
    reduce = Reduce(att, blocks, out, to_right, to_left, at_right, at_left,
                    r_send, r_recv, l_send, l_recv)
    attention = Attention(visible, ids, q, suffix, ka, va, qa, scores, att)

    barrier = pltpu.get_barrier_semaphore()
    for peer in tiles.peers:
        pl.semaphore_signal(barrier, inc=1, device_id=(peer, z), device_id_type=MESH)
    for way in (reduce.right, reduce.left):
        pl.semaphore_signal(barrier, inc=1, device_id=(me, way[4]), device_id_type=MESH)
    tiles.plan()
    loads[0].wait()
    tiles.cut()
    loads[1].wait()
    pl.semaphore_wait(barrier, GROUPS + 1)

    tiles.request()
    weights.start()
    tiles.pieces()
    attention.fixed()
    tiles.answer()
    weights.ring()
    tiles.spread()
    loads[2].wait()
    loads[3].wait()
    attention.bias(0)
    weights.opposite()
    weights.across(0)
    tiles.receive()
    attention.take(tiles)
    attention.score(0)
    beside = {
        0: [(weights.across, 1)],
        1: [(weights.across, 2)],
        2: [(weights.across, 3)],
        4: [(weights.last, 0)],
        6: [(weights.last, 1)],
        8: [(weights.last, 2)],
        10: [(weights.last, 3)],
    }
    for i in range(4 * NBLK):
        attention.pair(i)
        for step, *j in beside.get(i, ()):
            step(*j)
        if i == 11:
            weights.finish()
            reduce.stage(4, 0, NBLK - 1)
    reduce.stage(4, NBLK - 1, NBLK)
    for k in (3, 2, 1, 0):
        reduce.stage(k)
    reduce.drain()
    weights.drain()
    tiles.drain()


def layer(reads, visible, prefix, q, suffix, ids, w):
    smem = pl.BlockSpec(memory_space=pltpu.SMEM)
    vmem = pl.BlockSpec(memory_space=pltpu.VMEM)
    hbm = pl.BlockSpec(memory_space=pl.ANY)
    dma = pltpu.SemaphoreType.DMA
    return pl.pallas_call(
        layer_kernel,
        out_shape=jax.ShapeDtypeStruct((TOK, COLS), BF16),
        in_specs=[smem, smem, hbm, hbm, hbm, vmem, hbm],
        out_specs=vmem,
        scratch_shapes=[
            pltpu.VMEM((TPS, TILE, 2 * HEAD), BF16),
            pltpu.VMEM((TOK, HEADS * HEAD), BF16),
            pltpu.VMEM((TOK, 2 * HEAD), BF16),
            dma((4,)),
            pltpu.VMEM((GROUPS, HEADS * HEAD, HEAD), BF16),
            dma((36,)),
            dma((36,)),
            pltpu.VMEM((1, 128), jnp.int32),
            pltpu.VMEM((GROUPS, 1, 128), jnp.int32),
            pltpu.SMEM((GROUPS, 1, 128), jnp.int32),
            pltpu.VMEM((GROUPS - 1, 2 * TILE, HEAD), BF16),
            pltpu.VMEM((GROUPS + 1, 2 * TILE, HEAD), BF16),
            pltpu.VMEM((2 * TILE, HEAD), BF16),
            pltpu.VMEM((GROUPS, 16, HEAD), BF16),
            dma((3,)),
            dma((3,)),
            dma((8,)),
            dma((8,)),
            dma,
            pltpu.VMEM((2, 2 * HEAD, KEYS), BF16),
            pltpu.VMEM((2, KEYS, 2 * HEAD), BF16),
            pltpu.VMEM((2, PAIR, 2 * HEAD), BF16),
            pltpu.VMEM((2, PAIR, KEYS), F32),
            pltpu.VMEM((TOK, HEADS * HEAD), BF16),
            pltpu.VMEM((4, TOK, COLS), BF16),
            pltpu.VMEM((4, TOK, COLS), BF16),
            pltpu.VMEM((4, TOK, COLS), BF16),
            pltpu.VMEM((4, TOK, COLS), BF16),
            dma((4, NBLK)),
            dma((4, NBLK)),
            dma((4, NBLK)),
            dma((4, NBLK)),
        ],
        name="fetch_attend_project_reduce",
        compiler_params=pltpu.CompilerParams(
            collective_id=0, has_side_effects=True, vmem_limit_bytes=VMEM
        ),
    )(reads, visible, prefix, q, suffix, ids, w)


def local(queries, suffix_kv, prefix_key_value, answer_ids, read_tiles, visible, out_weight):
    return layer(read_tiles, visible, prefix_key_value, queries, suffix_kv, answer_ids,
                 out_weight)


def solution(mesh):
    placed = (
        P("dp", "tensor"),
        P("dp", "tensor"),
        P("dp", None, "tensor"),
        P("dp", None),
        P("dp", None),
        P("dp", None, None),
        P("tensor", "dp"),
    )
    return jax.shard_map(
        local, mesh=mesh, in_specs=placed, out_specs=P("dp", "tensor"), check_vma=False
    )
```

```python
import functools

import jax
import jax.numpy as jnp
from jax import lax
from jax.experimental import pallas as pl
from jax.experimental.pallas import tpu as pltpu
from jax.sharding import PartitionSpec as P

HEAD = 128
TILE = 64
READS = 26
GROUPS = 32
TPS = 8
TOK = 512
HEADS = 8
BLK = 128
NBLK = TOK // BLK
PRE = READS * TILE
KEYS = PRE + 2 * BLK
NZ = 8
COLS = 512
VMEM = 63 << 20
MESH = pl.DeviceIdType.MESH
PAIR = 2 * BLK
BF16 = jnp.bfloat16
F32 = jnp.float32
BIG = -1e30
LOG2E = 1.4426950408889634
SCALE = HEAD ** (-0.5) * LOG2E


def coords():
    g = lax.axis_index("dp")
    return g // 8, lax.rem(g // 2, 4), lax.rem(g, 2), lax.axis_index("tensor")


def place(x, y, c):
    return lax.rem(x, 4) * 8 + lax.rem(y, 4) * 2 + lax.rem(c, 2)


def remote(src, dst, send, recv, dp, tensor):
    return pltpu.make_async_remote_copy(
        src_ref=src, dst_ref=dst, send_sem=send, recv_sem=recv,
        device_id=(dp, tensor), device_id_type=MESH,
    )


class Tiles:
    def __init__(self, reads, prefix, ask, table, asked, packed, got, hot_out, hot_recv,
                 sem_send, sem_recv, spread_send, spread_recv, local_sem):
        self.reads, self.prefix, self.ask, self.table, self.asked = reads, prefix, ask, table, asked
        self.packed, self.got, self.hot_out, self.hot_recv = packed, got, hot_out, hot_recv
        self.sem_send, self.sem_recv, self.local_sem = sem_send, sem_recv, local_sem
        self.spread_send, self.spread_recv = spread_send, spread_recv
        self.x, self.y, self.c, self.z = coords()
        self.me = lax.axis_index("dp")
        self.peers = [place(self.x + k // 8, self.y + (k // 2) % 4, self.c + k % 2)
                      for k in range(1, GROUPS)]

    def plan(self):
        lane = lax.broadcasted_iota(jnp.int32, (1, 128), 1)
        first = jnp.full((1, 128), TPS, jnp.int32)
        last = jnp.full((1, 128), -1, jnp.int32)
        self.tiles = [self.reads[0, r] for r in range(READS)]
        for tile in self.tiles:
            here = lane == tile // TPS
            first = jnp.where(here, jnp.minimum(first, tile % TPS), first)
            last = jnp.where(here, jnp.maximum(last, tile % TPS), last)
        twice = last > first
        self.hot_owner = jnp.max(jnp.where(twice, lane, 0))
        self.hot_second = jnp.max(jnp.where(twice, last, 0))
        mine = jnp.where(first == TPS, 0, first)
        self.ask[...] = mine
        self.table[pl.ds(self.me, 1)] = mine[None]

    def cut(self):
        second = self.prefix[self.hot_second]
        self.hot_out[pl.ds(0, TILE)] = second[:, :HEAD]
        self.hot_out[pl.ds(TILE, TILE)] = second[:, HEAD:]
        self.part = pl.multiple_of(lax.rem(self.me, 8) * 16, 16)
        self.hot_recv[pl.ds(self.me, 1)] = self.hot_out[pl.ds(self.part, 16)][None]

    def request(self):
        for peer in self.peers:
            remote(self.ask, self.table.at[self.me], self.sem_send.at[0], self.sem_recv.at[0],
                   peer, self.z).start()

    def pieces(self):
        for peer in self.peers:
            part = pl.multiple_of(lax.rem(peer, 8) * 16, 16)
            remote(self.hot_out.at[pl.ds(part, 16)], self.hot_recv.at[self.me],
                   self.sem_send.at[1], self.sem_recv.at[1], peer, self.z).start()

    def wait_all(self, ref, sem):
        part = ref.at[pl.ds(0, GROUPS - 1)]
        pltpu.make_async_copy(part, part, sem).wait()

    def answer(self):
        me, z = self.me, self.z
        self.wait_all(self.table, self.sem_recv.at[0])
        load = pltpu.make_async_copy(self.table, self.asked, self.local_sem)
        load.start()
        load.wait()
        for k, peer in enumerate(self.peers):
            tile = self.prefix[self.asked[peer, 0, me]]
            self.packed[k, pl.ds(0, TILE)] = tile[:, :HEAD]
            self.packed[k, pl.ds(TILE, TILE)] = tile[:, HEAD:]
            remote(self.packed.at[k], self.got.at[me], self.sem_send.at[2],
                   self.sem_recv.at[2], peer, z).start()
        own = self.prefix[self.asked[me, 0, me]]
        self.got[pl.ds(me, 1), pl.ds(0, TILE)] = own[:, :HEAD][None]
        self.got[pl.ds(me, 1), pl.ds(TILE, TILE)] = own[:, HEAD:][None]

    def spread(self):
        self.wait_all(self.hot_recv, self.sem_recv.at[1])
        ref = self.got.at[GROUPS, pl.ds(self.part, 16)]
        self.got[GROUPS, pl.ds(self.part, 16)] = self.hot_recv[self.hot_owner]
        self.spreads = []
        for k in range(1, 8):
            copy = remote(ref, ref, self.spread_send.at[k], self.spread_recv.at[k],
                          place(self.x, self.y + k // 2, self.c + k % 2), self.z)
            copy.start()
            self.spreads.append(copy)

    def receive(self):
        self.wait_all(self.got, self.sem_recv.at[2])
        for copy in self.spreads:
            copy.wait_recv()

    def tile(self, r):
        owner = self.tiles[r] // TPS
        second = (owner == self.hot_owner) & (self.tiles[r] % TPS == self.hot_second)
        return self.got[jnp.where(second, GROUPS, owner)]

    def drain(self):
        self.wait_all(self.table, self.sem_send.at[0])
        self.wait_all(self.hot_recv, self.sem_send.at[1])
        self.wait_all(self.packed, self.sem_send.at[2])
        for copy in self.spreads:
            copy.wait_send()


class Weights:
    def __init__(self, blocks, send, recv):
        self.blocks, self.send, self.recv = blocks, send, recv
        self.x, self.y, self.c, self.z = coords()
        c = self.c
        x_mate, y_mate = 1 + 2 * lax.rem(self.x, 2), 1 + 2 * lax.rem(self.y, 2)
        first = x_mate * (1 - c) + y_mate * c
        second = y_mate * (1 - c) + x_mate * c
        self.f, self.s = (0, first, 4 - first, 2), (0, second, 4 - second, 2)
        self.sibling = place(self.x, self.y, c + 1)

    def at(self, jf, js):
        c = self.c
        f, s = self.f[jf], self.s[js]
        return place(self.x + f * (1 - c) + s * c, self.y + s * (1 - c) + f * c, c)

    def other_core(self, jf, js):
        c = 1 - self.c
        f, s = self.s[jf], self.f[js]
        return place(self.x + f * (1 - c) + s * c, self.y + s * (1 - c) + f * c, c)

    def copy(self, kind, block, dp, rows=None):
        ref = self.blocks.at[block]
        if rows is not None:
            ref = ref.at[pl.ds(rows * 512, 512)]
        return remote(ref, ref, self.send.at[kind], self.recv.at[kind], dp, self.z)

    def sent(self, kind):
        if kind < 2:
            return self.copy(kind, self.at(0, 0), self.at(kind + 1, 0))
        if kind < 4:
            return self.copy(kind, self.at(kind - 1, 0), self.at(4 - kind, 0), rows=kind - 2)
        if kind < 12:
            j, way = (kind - 4) // 2, kind % 2
            return self.copy(kind, self.at(j, 0), self.at(0, 1 + way))
        if kind < 20:
            j, way = (kind - 12) // 2, kind % 2
            return self.copy(kind, self.at(j, 1 + way), self.at(0, 2 - way), rows=way)
        return self.copy(kind, self.at((kind - 20) // 4, kind % 4), self.sibling)

    def go(self, *kinds):
        for kind in kinds:
            self.sent(kind).start()

    def come(self, *kinds):
        me = self.at(0, 0)
        for kind in kinds:
            if kind < 2:
                copy = self.copy(kind, self.at(kind + 1, 0), me)
            elif kind < 4:
                copy = self.copy(kind, self.at(3, 0), me, rows=kind - 2)
            elif kind < 12:
                copy = self.copy(kind, self.at((kind - 4) // 2, 1 + kind % 2), me)
            elif kind < 20:
                copy = self.copy(kind, self.at((kind - 12) // 2, 3), me, rows=kind % 2)
            else:
                copy = self.copy(kind, self.other_core((kind - 20) // 4, kind % 4), me)
            copy.wait_recv()

    def start(self):
        self.go(0, 1, 4, 5, 20)

    def ring(self):
        self.come(0)
        self.go(2, 6, 7, 24)
        self.come(1)
        self.go(3, 8, 9, 28)

    def opposite(self):
        self.come(2, 3)
        self.go(10, 11, 32)

    def across(self, j):
        self.come(4 + 2 * j, 5 + 2 * j)
        self.go(12 + 2 * j, 13 + 2 * j, 21 + 4 * j, 22 + 4 * j)

    def last(self, j):
        self.come(12 + 2 * j, 13 + 2 * j)
        self.go(23 + 4 * j)

    def finish(self):
        self.come(*range(20, 36))

    def drain(self):
        for kind in range(36):
            self.sent(kind).wait_send()


class Reduce:
    def __init__(self, att, blocks, out, to_right, to_left, at_right, at_left,
                 r_send, r_recv, l_send, l_recv):
        self.att, self.blocks, self.out = att, blocks, out
        self.me, self.z = lax.axis_index("dp"), lax.axis_index("tensor")
        right, left = lax.rem(self.z + 1, NZ), lax.rem(self.z + NZ - 1, NZ)
        self.right = (to_right, at_right, r_send, r_recv, right)
        self.left = (to_left, at_left, l_send, l_recv, left)

    def rows(self, b):
        return pl.ds(pl.multiple_of(b * BLK, BLK), BLK)

    def project(self, b, hops):
        base = lax.rem(self.z + NZ + hops, NZ) * 4
        wide = jnp.concatenate([self.blocks[base + i] for i in range(4)], axis=1)
        return jnp.dot(self.att[self.rows(b), :], wide, preferred_element_type=F32)

    def copy(self, way, k, b):
        to, at, send, recv, peer = way
        part = (k - 1, self.rows(b), pl.ds(0, COLS // 2 if k == 4 else COLS))
        return remote(to.at[part], at.at[part], send.at[k - 1, b], recv.at[k - 1, b],
                      self.me, peer)

    def send(self, way, k, b, value):
        way[0][k - 1, self.rows(b), pl.ds(0, value.shape[1])] = value.astype(BF16)
        self.copy(way, k, b).start()

    def arrived(self, way, k, b):
        self.copy(way, k + 1, b).wait_recv()
        return way[1][k, self.rows(b), pl.ds(0, COLS // 2 if k == 3 else COLS)].astype(F32)

    def stage(self, k, first=0, end=NBLK):
        half = COLS // 2

        def body(b, _):
            if k == 4:
                part = self.project(b, 4)
                self.send(self.right, 4, b, part[:, :half])
                self.send(self.left, 4, b, part[:, half:])
            elif k == 0:
                part = self.project(b, 0)
                part = part + self.arrived(self.right, 0, b)
                part = part + self.arrived(self.left, 0, b)
                self.out[self.rows(b), :] = part.astype(BF16)
            else:
                for way, hops in ((self.right, k), (self.left, -k)):
                    part = self.project(b, hops)
                    come = self.arrived(way, k, b)
                    if k == 3 and hops > 0:
                        part = jnp.concatenate([part[:, :half] + come, part[:, half:]], axis=1)
                    elif k == 3:
                        part = jnp.concatenate([part[:, :half], part[:, half:] + come], axis=1)
                    else:
                        part = part + come
                    self.send(way, k, b, part)
            return 0

        lax.fori_loop(first, end, body, 0)

    def drain(self):
        def body(b, _):
            for k in range(1, 5):
                self.copy(self.right, k, b).wait_send()
                self.copy(self.left, k, b).wait_send()
            return 0

        lax.fori_loop(0, NBLK, body, 0)


class Attention:
    def __init__(self, visible, ids, q, suffix, ka, va, qa, scores, att):
        self.visible, self.ids, self.q, self.suffix = visible, ids, q, suffix
        self.ka, self.va, self.qa, self.scores, self.att = ka, va, qa, scores, att

    def fixed(self):
        row = lax.broadcasted_iota(jnp.int32, (BLK, BLK), 0)
        col = lax.broadcasted_iota(jnp.int32, (BLK, BLK), 1)
        self.row, self.col = row, col
        eye = jnp.where(row == col, 1.0, 0.0).astype(BF16)
        for slot in range(2):
            for j in range(2):
                self.qa[slot, pl.ds(j * BLK, BLK), pl.ds(HEAD, HEAD)] = eye
            self.va[slot, :, pl.ds(HEAD, HEAD)] = jnp.ones((KEYS, HEAD), BF16)
        self.down = [jnp.broadcast_to(self.ids[:, pl.ds(b * BLK, BLK)].astype(F32), (BLK, BLK)).T
                     for b in range(NBLK)]

    def bias(self, b):
        slot = b % 2
        second = self.down[b] >= 8.0
        for r in range(0, READS, 2):
            lines = [jnp.where(self.col < TILE,
                               jnp.where(self.visible[0, n, r] > 0, 0.0, BIG),
                               jnp.where(self.visible[0, n, r + 1] > 0, 0.0, BIG))
                     for n in range(2)]
            self.ka[slot, pl.ds(HEAD, HEAD), pl.ds(r * TILE, BLK)] = jnp.where(
                second, lines[1], lines[0]).astype(BF16)
        start = max(b - 1, 0) * BLK
        for part in range(2):
            base = start + part * BLK
            at = pl.ds(PRE + part * BLK, BLK)
            same = self.down[b] == self.ids[:, pl.ds(base, BLK)].astype(F32)
            seen = same & (self.col + base <= self.row + b * BLK)
            self.ka[slot, pl.ds(HEAD, HEAD), at] = jnp.where(seen, 0.0, BIG).astype(BF16)
            self.ka[slot, pl.ds(0, HEAD), at] = self.suffix[pl.ds(base, BLK), pl.ds(0, HEAD)].T
            self.va[slot, at, pl.ds(0, HEAD)] = self.suffix[pl.ds(base, BLK), pl.ds(HEAD, HEAD)]

    def take(self, tiles):
        for r in range(0, READS, 2):
            one, two = tiles.tile(r), tiles.tile(r + 1)
            across = jnp.concatenate([one[:TILE], two[:TILE]], axis=0).T
            for slot in range(2):
                self.ka[slot, pl.ds(0, HEAD), pl.ds(r * TILE, BLK)] = across
                self.va[slot, pl.ds(r * TILE, TILE), pl.ds(0, HEAD)] = one[TILE:]
                self.va[slot, pl.ds((r + 1) * TILE, TILE), pl.ds(0, HEAD)] = two[TILE:]

    def score(self, i):
        b, h = i // 4, i % 4 * 2
        for j in range(2):
            self.qa[i % 2, pl.ds(j * BLK, BLK), pl.ds(0, HEAD)] = (
                self.q[pl.ds(b * BLK, BLK), pl.ds((h + j) * HEAD, HEAD)])
        self.scores[i % 2] = jnp.dot(self.qa[i % 2], self.ka[b % 2], preferred_element_type=F32)

    def rest(self, i):
        b, h = i // 4, i % 4 * 2
        scores = self.scores[i % 2]
        top = jnp.max(scores, axis=1, keepdims=True)
        probs = jnp.exp2((scores - top) * SCALE).astype(BF16)
        mixed = jnp.dot(probs, self.va[b % 2], preferred_element_type=F32)
        done = (mixed[:, :HEAD] / mixed[:, HEAD:]).astype(BF16)
        for j in range(2):
            self.att[pl.ds(b * BLK, BLK), pl.ds((h + j) * HEAD, HEAD)] = done[j * BLK:(j + 1) * BLK]

    def pair(self, i):
        if i % 4 == 3 and i + 1 < 4 * NBLK:
            self.bias(i // 4 + 1)
        if i + 1 < 4 * NBLK:
            self.score(i + 1)
        self.rest(i)


def layer_kernel(reads, visible, prefix_hbm, q_hbm, suffix_hbm, ids, w_hbm, out,
                 prefix, q, suffix, load_sem, blocks, w_send, w_recv,
                 ask, table, asked, packed, got, hot_out, hot_recv,
                 t_send, t_recv, spread_send, spread_recv, local_sem,
                 ka, va, qa, scores, att,
                 to_right, to_left, at_right, at_left, r_send, r_recv, l_send, l_recv):
    me, z = lax.axis_index("dp"), lax.axis_index("tensor")
    loads = [pltpu.make_async_copy(src, dst, load_sem.at[i]) for i, (src, dst) in enumerate(
        ((prefix_hbm, prefix), (w_hbm, blocks.at[me]), (suffix_hbm, suffix), (q_hbm, q)))]
    for load in loads:
        load.start()
    tiles = Tiles(reads, prefix, ask, table, asked, packed, got, hot_out, hot_recv,
                  t_send, t_recv, spread_send, spread_recv, local_sem)
    weights = Weights(blocks, w_send, w_recv)
    reduce = Reduce(att, blocks, out, to_right, to_left, at_right, at_left,
                    r_send, r_recv, l_send, l_recv)
    attention = Attention(visible, ids, q, suffix, ka, va, qa, scores, att)

    barrier = pltpu.get_barrier_semaphore()
    for peer in tiles.peers:
        pl.semaphore_signal(barrier, inc=1, device_id=(peer, z), device_id_type=MESH)
    for way in (reduce.right, reduce.left):
        pl.semaphore_signal(barrier, inc=1, device_id=(me, way[4]), device_id_type=MESH)
    tiles.plan()
    loads[0].wait()
    tiles.cut()
    loads[1].wait()
    pl.semaphore_wait(barrier, GROUPS + 1)

    tiles.request()
    weights.start()
    tiles.pieces()
    attention.fixed()
    tiles.answer()
    weights.ring()
    tiles.spread()
    loads[2].wait()
    loads[3].wait()
    attention.bias(0)
    weights.opposite()
    weights.across(0)
    tiles.receive()
    attention.take(tiles)
    attention.score(0)
    beside = {
        0: [(weights.across, 1)],
        1: [(weights.across, 2)],
        2: [(weights.across, 3)],
        4: [(weights.last, 0)],
        6: [(weights.last, 1)],
        8: [(weights.last, 2)],
        10: [(weights.last, 3)],
    }
    for i in range(4 * NBLK):
        attention.pair(i)
        for step, *j in beside.get(i, ()):
            step(*j)
        if i == 11:
            weights.finish()
            reduce.stage(4, 0, NBLK - 1)
        if i == 13:
            reduce.stage(3, 0, 2)
    reduce.stage(4, NBLK - 1, NBLK)
    reduce.stage(3, 2, NBLK)
    for k in (2, 1, 0):
        reduce.stage(k)
    reduce.drain()
    weights.drain()
    tiles.drain()


def layer(reads, visible, prefix, q, suffix, ids, w):
    smem = pl.BlockSpec(memory_space=pltpu.SMEM)
    vmem = pl.BlockSpec(memory_space=pltpu.VMEM)
    hbm = pl.BlockSpec(memory_space=pl.ANY)
    dma = pltpu.SemaphoreType.DMA
    return pl.pallas_call(
        layer_kernel,
        out_shape=jax.ShapeDtypeStruct((TOK, COLS), BF16),
        in_specs=[smem, smem, hbm, hbm, hbm, vmem, hbm],
        out_specs=vmem,
        scratch_shapes=[
            pltpu.VMEM((TPS, TILE, 2 * HEAD), BF16),
            pltpu.VMEM((TOK, HEADS * HEAD), BF16),
            pltpu.VMEM((TOK, 2 * HEAD), BF16),
            dma((4,)),
            pltpu.VMEM((GROUPS, HEADS * HEAD, HEAD), BF16),
            dma((36,)),
            dma((36,)),
            pltpu.VMEM((1, 128), jnp.int32),
            pltpu.VMEM((GROUPS, 1, 128), jnp.int32),
            pltpu.SMEM((GROUPS, 1, 128), jnp.int32),
            pltpu.VMEM((GROUPS - 1, 2 * TILE, HEAD), BF16),
            pltpu.VMEM((GROUPS + 1, 2 * TILE, HEAD), BF16),
            pltpu.VMEM((2 * TILE, HEAD), BF16),
            pltpu.VMEM((GROUPS, 16, HEAD), BF16),
            dma((3,)),
            dma((3,)),
            dma((8,)),
            dma((8,)),
            dma,
            pltpu.VMEM((2, 2 * HEAD, KEYS), BF16),
            pltpu.VMEM((2, KEYS, 2 * HEAD), BF16),
            pltpu.VMEM((2, PAIR, 2 * HEAD), BF16),
            pltpu.VMEM((2, PAIR, KEYS), F32),
            pltpu.VMEM((TOK, HEADS * HEAD), BF16),
            pltpu.VMEM((4, TOK, COLS), BF16),
            pltpu.VMEM((4, TOK, COLS), BF16),
            pltpu.VMEM((4, TOK, COLS), BF16),
            pltpu.VMEM((4, TOK, COLS), BF16),
            dma((4, NBLK)),
            dma((4, NBLK)),
            dma((4, NBLK)),
            dma((4, NBLK)),
        ],
        name="fetch_attend_project_reduce",
        compiler_params=pltpu.CompilerParams(
            collective_id=0, has_side_effects=True, vmem_limit_bytes=VMEM
        ),
    )(reads, visible, prefix, q, suffix, ids, w)


def local(queries, suffix_kv, prefix_key_value, answer_ids, read_tiles, visible, out_weight):
    return layer(read_tiles, visible, prefix_key_value, queries, suffix_kv, answer_ids,
                 out_weight)


def solution(mesh):
    placed = (
        P("dp", "tensor"),
        P("dp", "tensor"),
        P("dp", None, "tensor"),
        P("dp", None),
        P("dp", None),
        P("dp", None, None),
        P("tensor", "dp"),
    )
    return jax.shard_map(
        local, mesh=mesh, in_specs=placed, out_specs=P("dp", "tensor"), check_vma=False
    )
```

```python
import functools

import jax
import jax.numpy as jnp
from jax import lax
from jax.experimental import pallas as pl
from jax.experimental.pallas import tpu as pltpu
from jax.sharding import PartitionSpec as P

HEAD = 128
TILE = 64
READS = 26
GROUPS = 32
TPS = 8
TOK = 512
HEADS = 8
BLK = 128
NBLK = TOK // BLK
PRE = READS * TILE
KEYS = PRE + 2 * BLK
NZ = 8
COLS = 512
VMEM = 63 << 20
MESH = pl.DeviceIdType.MESH
PAIR = 2 * BLK
BF16 = jnp.bfloat16
F32 = jnp.float32
BIG = -1e30
LOG2E = 1.4426950408889634
SCALE = HEAD ** (-0.5) * LOG2E


def coords():
    g = lax.axis_index("dp")
    return g // 8, lax.rem(g // 2, 4), lax.rem(g, 2), lax.axis_index("tensor")


def place(x, y, c):
    return lax.rem(x, 4) * 8 + lax.rem(y, 4) * 2 + lax.rem(c, 2)


def remote(src, dst, send, recv, dp, tensor):
    return pltpu.make_async_remote_copy(
        src_ref=src, dst_ref=dst, send_sem=send, recv_sem=recv,
        device_id=(dp, tensor), device_id_type=MESH,
    )


def far_first(k):
    x, y = k // 8, k // 2 % 4
    return -min(x, 4 - x) - min(y, 4 - y), k * 11 % GROUPS


class Tiles:
    def __init__(self, reads, prefix, ask, table, asked, packed, got, hot_out, hot_recv,
                 sem_send, sem_recv, spread_send, spread_recv, local_sem):
        self.reads, self.prefix, self.ask, self.table, self.asked = reads, prefix, ask, table, asked
        self.packed, self.got, self.hot_out, self.hot_recv = packed, got, hot_out, hot_recv
        self.sem_send, self.sem_recv, self.local_sem = sem_send, sem_recv, local_sem
        self.spread_send, self.spread_recv = spread_send, spread_recv
        self.x, self.y, self.c, self.z = coords()
        self.me = lax.axis_index("dp")
        self.peers = [place(self.x + k // 8, self.y + (k // 2) % 4, self.c + k % 2)
                      for k in sorted(range(1, GROUPS), key=far_first)]

    def plan(self):
        lane = lax.broadcasted_iota(jnp.int32, (1, 128), 1)
        first = jnp.full((1, 128), TPS, jnp.int32)
        last = jnp.full((1, 128), -1, jnp.int32)
        self.tiles = [self.reads[0, r] for r in range(READS)]
        for tile in self.tiles:
            here = lane == tile // TPS
            first = jnp.where(here, jnp.minimum(first, tile % TPS), first)
            last = jnp.where(here, jnp.maximum(last, tile % TPS), last)
        twice = last > first
        self.hot_owner = jnp.max(jnp.where(twice, lane, 0))
        self.hot_second = jnp.max(jnp.where(twice, last, 0))
        mine = jnp.where(first == TPS, 0, first)
        self.ask[...] = mine
        self.table[pl.ds(self.me, 1)] = mine[None]

    def cut(self):
        second = self.prefix[self.hot_second]
        self.hot_out[pl.ds(0, TILE)] = second[:, :HEAD]
        self.hot_out[pl.ds(TILE, TILE)] = second[:, HEAD:]
        self.part = pl.multiple_of(lax.rem(self.me, 8) * 16, 16)
        self.hot_recv[pl.ds(self.me, 1)] = self.hot_out[pl.ds(self.part, 16)][None]

    def request(self):
        for peer in self.peers:
            remote(self.ask, self.table.at[self.me], self.sem_send.at[0], self.sem_recv.at[0],
                   peer, self.z).start()

    def pieces(self):
        for peer in self.peers:
            part = pl.multiple_of(lax.rem(peer, 8) * 16, 16)
            remote(self.hot_out.at[pl.ds(part, 16)], self.hot_recv.at[self.me],
                   self.sem_send.at[1], self.sem_recv.at[1], peer, self.z).start()

    def wait_all(self, ref, sem):
        part = ref.at[pl.ds(0, GROUPS - 1)]
        pltpu.make_async_copy(part, part, sem).wait()

    def answer(self):
        me, z = self.me, self.z
        self.wait_all(self.table, self.sem_recv.at[0])
        load = pltpu.make_async_copy(self.table, self.asked, self.local_sem)
        load.start()
        load.wait()
        for k, peer in enumerate(self.peers):
            tile = self.prefix[self.asked[peer, 0, me]]
            self.packed[k, pl.ds(0, TILE)] = tile[:, :HEAD]
            self.packed[k, pl.ds(TILE, TILE)] = tile[:, HEAD:]
            remote(self.packed.at[k], self.got.at[me], self.sem_send.at[2],
                   self.sem_recv.at[2], peer, z).start()
        own = self.prefix[self.asked[me, 0, me]]
        self.got[pl.ds(me, 1), pl.ds(0, TILE)] = own[:, :HEAD][None]
        self.got[pl.ds(me, 1), pl.ds(TILE, TILE)] = own[:, HEAD:][None]

    def spread(self):
        self.wait_all(self.hot_recv, self.sem_recv.at[1])
        ref = self.got.at[GROUPS, pl.ds(self.part, 16)]
        self.got[GROUPS, pl.ds(self.part, 16)] = self.hot_recv[self.hot_owner]
        self.spreads = []
        for k in range(1, 8):
            copy = remote(ref, ref, self.spread_send.at[k], self.spread_recv.at[k],
                          place(self.x, self.y + k // 2, self.c + k % 2), self.z)
            copy.start()
            self.spreads.append(copy)

    def receive(self):
        self.wait_all(self.got, self.sem_recv.at[2])
        for copy in self.spreads:
            copy.wait_recv()

    def tile(self, r):
        owner = self.tiles[r] // TPS
        second = (owner == self.hot_owner) & (self.tiles[r] % TPS == self.hot_second)
        return self.got[jnp.where(second, GROUPS, owner)]

    def drain(self):
        self.wait_all(self.table, self.sem_send.at[0])
        self.wait_all(self.hot_recv, self.sem_send.at[1])
        self.wait_all(self.packed, self.sem_send.at[2])
        for copy in self.spreads:
            copy.wait_send()


class Weights:
    def __init__(self, blocks, send, recv):
        self.blocks, self.send, self.recv = blocks, send, recv
        self.x, self.y, self.c, self.z = coords()
        c = self.c
        x_mate, y_mate = 1 + 2 * lax.rem(self.x, 2), 1 + 2 * lax.rem(self.y, 2)
        first = x_mate * (1 - c) + y_mate * c
        second = y_mate * (1 - c) + x_mate * c
        self.f, self.s = (0, first, 4 - first, 2), (0, second, 4 - second, 2)
        self.sibling = place(self.x, self.y, c + 1)

    def at(self, jf, js):
        c = self.c
        f, s = self.f[jf], self.s[js]
        return place(self.x + f * (1 - c) + s * c, self.y + s * (1 - c) + f * c, c)

    def other_core(self, jf, js):
        c = 1 - self.c
        f, s = self.s[jf], self.f[js]
        return place(self.x + f * (1 - c) + s * c, self.y + s * (1 - c) + f * c, c)

    def copy(self, kind, block, dp, rows=None):
        ref = self.blocks.at[block]
        if rows is not None:
            ref = ref.at[pl.ds(rows * 512, 512)]
        return remote(ref, ref, self.send.at[kind], self.recv.at[kind], dp, self.z)

    def sent(self, kind):
        if kind < 2:
            return self.copy(kind, self.at(0, 0), self.at(kind + 1, 0))
        if kind < 4:
            return self.copy(kind, self.at(kind - 1, 0), self.at(4 - kind, 0), rows=kind - 2)
        if kind < 12:
            j, way = (kind - 4) // 2, kind % 2
            return self.copy(kind, self.at(j, 0), self.at(0, 1 + way))
        if kind < 20:
            j, way = (kind - 12) // 2, kind % 2
            return self.copy(kind, self.at(j, 1 + way), self.at(0, 2 - way), rows=way)
        return self.copy(kind, self.at((kind - 20) // 4, kind % 4), self.sibling)

    def go(self, *kinds):
        for kind in kinds:
            self.sent(kind).start()

    def come(self, *kinds):
        me = self.at(0, 0)
        for kind in kinds:
            if kind < 2:
                copy = self.copy(kind, self.at(kind + 1, 0), me)
            elif kind < 4:
                copy = self.copy(kind, self.at(3, 0), me, rows=kind - 2)
            elif kind < 12:
                copy = self.copy(kind, self.at((kind - 4) // 2, 1 + kind % 2), me)
            elif kind < 20:
                copy = self.copy(kind, self.at((kind - 12) // 2, 3), me, rows=kind % 2)
            else:
                copy = self.copy(kind, self.other_core((kind - 20) // 4, kind % 4), me)
            copy.wait_recv()

    def start(self):
        self.go(0, 1, 4, 5, 20)

    def ring(self):
        self.come(0)
        self.go(2, 6, 7, 24)
        self.come(1)
        self.go(3, 8, 9, 28)

    def opposite(self):
        self.come(2, 3)
        self.go(10, 11, 32)

    def across(self, j):
        self.come(4 + 2 * j, 5 + 2 * j)
        self.go(12 + 2 * j, 13 + 2 * j, 21 + 4 * j, 22 + 4 * j)

    def last(self, j):
        self.come(12 + 2 * j, 13 + 2 * j)
        self.go(23 + 4 * j)

    def finish(self):
        self.come(*range(20, 36))

    def drain(self):
        for kind in range(36):
            self.sent(kind).wait_send()


class Reduce:
    def __init__(self, att, blocks, out, to_right, to_left, at_right, at_left,
                 r_send, r_recv, l_send, l_recv):
        self.att, self.blocks, self.out = att, blocks, out
        self.me, self.z = lax.axis_index("dp"), lax.axis_index("tensor")
        right, left = lax.rem(self.z + 1, NZ), lax.rem(self.z + NZ - 1, NZ)
        self.right = (to_right, at_right, r_send, r_recv, right)
        self.left = (to_left, at_left, l_send, l_recv, left)

    def rows(self, b):
        return pl.ds(pl.multiple_of(b * BLK, BLK), BLK)

    def project(self, b, hops):
        base = lax.rem(self.z + NZ + hops, NZ) * 4
        wide = jnp.concatenate([self.blocks[base + i] for i in range(4)], axis=1)
        return jnp.dot(self.att[self.rows(b), :], wide, preferred_element_type=F32)

    def copy(self, way, k, b):
        to, at, send, recv, peer = way
        part = (k - 1, self.rows(b), pl.ds(0, COLS // 2 if k == 4 else COLS))
        return remote(to.at[part], at.at[part], send.at[k - 1, b], recv.at[k - 1, b],
                      self.me, peer)

    def send(self, way, k, b, value):
        way[0][k - 1, self.rows(b), pl.ds(0, value.shape[1])] = value.astype(BF16)
        self.copy(way, k, b).start()

    def arrived(self, way, k, b):
        self.copy(way, k + 1, b).wait_recv()
        return way[1][k, self.rows(b), pl.ds(0, COLS // 2 if k == 3 else COLS)].astype(F32)

    def stage(self, k, first=0, end=NBLK):
        half = COLS // 2

        def body(b, _):
            if k == 4:
                part = self.project(b, 4)
                self.send(self.right, 4, b, part[:, :half])
                self.send(self.left, 4, b, part[:, half:])
            elif k == 0:
                part = self.project(b, 0)
                part = part + self.arrived(self.right, 0, b)
                part = part + self.arrived(self.left, 0, b)
                self.out[self.rows(b), :] = part.astype(BF16)
            else:
                for way, hops in ((self.right, k), (self.left, -k)):
                    part = self.project(b, hops)
                    come = self.arrived(way, k, b)
                    if k == 3 and hops > 0:
                        part = jnp.concatenate([part[:, :half] + come, part[:, half:]], axis=1)
                    elif k == 3:
                        part = jnp.concatenate([part[:, :half], part[:, half:] + come], axis=1)
                    else:
                        part = part + come
                    self.send(way, k, b, part)
            return 0

        lax.fori_loop(first, end, body, 0)

    def drain(self):
        def body(b, _):
            for k in range(1, 5):
                self.copy(self.right, k, b).wait_send()
                self.copy(self.left, k, b).wait_send()
            return 0

        lax.fori_loop(0, NBLK, body, 0)


class Attention:
    def __init__(self, visible, ids, q, suffix, ka, va, qa, scores, att):
        self.visible, self.ids, self.q, self.suffix = visible, ids, q, suffix
        self.ka, self.va, self.qa, self.scores, self.att = ka, va, qa, scores, att

    def fixed(self):
        row = lax.broadcasted_iota(jnp.int32, (BLK, BLK), 0)
        col = lax.broadcasted_iota(jnp.int32, (BLK, BLK), 1)
        self.row, self.col = row, col
        eye = jnp.where(row == col, 1.0, 0.0).astype(BF16)
        for slot in range(2):
            for j in range(2):
                self.qa[slot, pl.ds(j * BLK, BLK), pl.ds(HEAD, HEAD)] = eye
            self.va[slot, :, pl.ds(HEAD, HEAD)] = jnp.ones((KEYS, HEAD), BF16)
        self.down = [jnp.broadcast_to(self.ids[:, pl.ds(b * BLK, BLK)].astype(F32), (BLK, BLK)).T
                     for b in range(NBLK)]

    def bias(self, b):
        slot = b % 2
        second = self.down[b] >= 8.0
        for r in range(0, READS, 2):
            lines = [jnp.where(self.col < TILE,
                               jnp.where(self.visible[0, n, r] > 0, 0.0, BIG),
                               jnp.where(self.visible[0, n, r + 1] > 0, 0.0, BIG))
                     for n in range(2)]
            self.ka[slot, pl.ds(HEAD, HEAD), pl.ds(r * TILE, BLK)] = jnp.where(
                second, lines[1], lines[0]).astype(BF16)
        start = max(b - 1, 0) * BLK
        for part in range(2):
            base = start + part * BLK
            at = pl.ds(PRE + part * BLK, BLK)
            same = self.down[b] == self.ids[:, pl.ds(base, BLK)].astype(F32)
            seen = same & (self.col + base <= self.row + b * BLK)
            self.ka[slot, pl.ds(HEAD, HEAD), at] = jnp.where(seen, 0.0, BIG).astype(BF16)
            self.ka[slot, pl.ds(0, HEAD), at] = self.suffix[pl.ds(base, BLK), pl.ds(0, HEAD)].T
            self.va[slot, at, pl.ds(0, HEAD)] = self.suffix[pl.ds(base, BLK), pl.ds(HEAD, HEAD)]

    def take(self, tiles):
        for r in range(0, READS, 2):
            one, two = tiles.tile(r), tiles.tile(r + 1)
            across = jnp.concatenate([one[:TILE], two[:TILE]], axis=0).T
            for slot in range(2):
                self.ka[slot, pl.ds(0, HEAD), pl.ds(r * TILE, BLK)] = across
                self.va[slot, pl.ds(r * TILE, TILE), pl.ds(0, HEAD)] = one[TILE:]
                self.va[slot, pl.ds((r + 1) * TILE, TILE), pl.ds(0, HEAD)] = two[TILE:]

    def score(self, i):
        b, h = i // 4, i % 4 * 2
        for j in range(2):
            self.qa[i % 2, pl.ds(j * BLK, BLK), pl.ds(0, HEAD)] = (
                self.q[pl.ds(b * BLK, BLK), pl.ds((h + j) * HEAD, HEAD)])
        self.scores[i % 2] = jnp.dot(self.qa[i % 2], self.ka[b % 2], preferred_element_type=F32)

    def rest(self, i):
        b, h = i // 4, i % 4 * 2
        scores = self.scores[i % 2]
        top = jnp.max(scores, axis=1, keepdims=True)
        probs = jnp.exp2((scores - top) * SCALE).astype(BF16)
        mixed = jnp.dot(probs, self.va[b % 2], preferred_element_type=F32)
        done = (mixed[:, :HEAD] / mixed[:, HEAD:]).astype(BF16)
        for j in range(2):
            self.att[pl.ds(b * BLK, BLK), pl.ds((h + j) * HEAD, HEAD)] = done[j * BLK:(j + 1) * BLK]

    def pair(self, i):
        if i % 4 == 3 and i + 1 < 4 * NBLK:
            self.bias(i // 4 + 1)
        if i + 1 < 4 * NBLK:
            self.score(i + 1)
        self.rest(i)


def layer_kernel(reads, visible, prefix_hbm, q_hbm, suffix_hbm, ids, w_hbm, out,
                 prefix, q, suffix, load_sem, blocks, w_send, w_recv,
                 ask, table, asked, packed, got, hot_out, hot_recv,
                 t_send, t_recv, spread_send, spread_recv, local_sem,
                 ka, va, qa, scores, att,
                 to_right, to_left, at_right, at_left, r_send, r_recv, l_send, l_recv):
    me, z = lax.axis_index("dp"), lax.axis_index("tensor")
    loads = [pltpu.make_async_copy(src, dst, load_sem.at[i]) for i, (src, dst) in enumerate(
        ((prefix_hbm, prefix), (w_hbm, blocks.at[me]), (suffix_hbm, suffix), (q_hbm, q)))]
    for load in loads:
        load.start()
    tiles = Tiles(reads, prefix, ask, table, asked, packed, got, hot_out, hot_recv,
                  t_send, t_recv, spread_send, spread_recv, local_sem)
    weights = Weights(blocks, w_send, w_recv)
    reduce = Reduce(att, blocks, out, to_right, to_left, at_right, at_left,
                    r_send, r_recv, l_send, l_recv)
    attention = Attention(visible, ids, q, suffix, ka, va, qa, scores, att)

    barrier = pltpu.get_barrier_semaphore()
    for peer in tiles.peers:
        pl.semaphore_signal(barrier, inc=1, device_id=(peer, z), device_id_type=MESH)
    for way in (reduce.right, reduce.left):
        pl.semaphore_signal(barrier, inc=1, device_id=(me, way[4]), device_id_type=MESH)
    tiles.plan()
    loads[0].wait()
    tiles.cut()
    loads[1].wait()
    pl.semaphore_wait(barrier, GROUPS + 1)

    tiles.request()
    weights.start()
    tiles.pieces()
    attention.fixed()
    tiles.answer()
    weights.ring()
    tiles.spread()
    loads[2].wait()
    loads[3].wait()
    attention.bias(0)
    weights.opposite()
    weights.across(0)
    tiles.receive()
    attention.take(tiles)
    attention.score(0)
    beside = {
        0: [(weights.across, 1)],
        1: [(weights.across, 2)],
        2: [(weights.across, 3)],
        4: [(weights.last, 0)],
        6: [(weights.last, 1)],
        8: [(weights.last, 2)],
        10: [(weights.last, 3)],
    }
    for i in range(4 * NBLK):
        attention.pair(i)
        for step, *j in beside.get(i, ()):
            step(*j)
        if i == 11:
            weights.finish()
            reduce.stage(4, 0, NBLK - 1)
        if i == 13:
            reduce.stage(3, 0, 2)
    reduce.stage(4, NBLK - 1, NBLK)
    reduce.stage(3, 2, NBLK)
    for k in (2, 1, 0):
        reduce.stage(k)
    reduce.drain()
    weights.drain()
    tiles.drain()


def layer(reads, visible, prefix, q, suffix, ids, w):
    smem = pl.BlockSpec(memory_space=pltpu.SMEM)
    vmem = pl.BlockSpec(memory_space=pltpu.VMEM)
    hbm = pl.BlockSpec(memory_space=pl.ANY)
    dma = pltpu.SemaphoreType.DMA
    return pl.pallas_call(
        layer_kernel,
        out_shape=jax.ShapeDtypeStruct((TOK, COLS), BF16),
        in_specs=[smem, smem, hbm, hbm, hbm, vmem, hbm],
        out_specs=vmem,
        scratch_shapes=[
            pltpu.VMEM((TPS, TILE, 2 * HEAD), BF16),
            pltpu.VMEM((TOK, HEADS * HEAD), BF16),
            pltpu.VMEM((TOK, 2 * HEAD), BF16),
            dma((4,)),
            pltpu.VMEM((GROUPS, HEADS * HEAD, HEAD), BF16),
            dma((36,)),
            dma((36,)),
            pltpu.VMEM((1, 128), jnp.int32),
            pltpu.VMEM((GROUPS, 1, 128), jnp.int32),
            pltpu.SMEM((GROUPS, 1, 128), jnp.int32),
            pltpu.VMEM((GROUPS - 1, 2 * TILE, HEAD), BF16),
            pltpu.VMEM((GROUPS + 1, 2 * TILE, HEAD), BF16),
            pltpu.VMEM((2 * TILE, HEAD), BF16),
            pltpu.VMEM((GROUPS, 16, HEAD), BF16),
            dma((3,)),
            dma((3,)),
            dma((8,)),
            dma((8,)),
            dma,
            pltpu.VMEM((2, 2 * HEAD, KEYS), BF16),
            pltpu.VMEM((2, KEYS, 2 * HEAD), BF16),
            pltpu.VMEM((2, PAIR, 2 * HEAD), BF16),
            pltpu.VMEM((2, PAIR, KEYS), F32),
            pltpu.VMEM((TOK, HEADS * HEAD), BF16),
            pltpu.VMEM((4, TOK, COLS), BF16),
            pltpu.VMEM((4, TOK, COLS), BF16),
            pltpu.VMEM((4, TOK, COLS), BF16),
            pltpu.VMEM((4, TOK, COLS), BF16),
            dma((4, NBLK)),
            dma((4, NBLK)),
            dma((4, NBLK)),
            dma((4, NBLK)),
        ],
        name="fetch_attend_project_reduce",
        compiler_params=pltpu.CompilerParams(
            collective_id=0, has_side_effects=True, vmem_limit_bytes=VMEM
        ),
    )(reads, visible, prefix, q, suffix, ids, w)


def local(queries, suffix_kv, prefix_key_value, answer_ids, read_tiles, visible, out_weight):
    return layer(read_tiles, visible, prefix_key_value, queries, suffix_kv, answer_ids,
                 out_weight)


def solution(mesh):
    placed = (
        P("dp", "tensor"),
        P("dp", "tensor"),
        P("dp", None, "tensor"),
        P("dp", None),
        P("dp", None),
        P("dp", None, None),
        P("tensor", "dp"),
    )
    return jax.shard_map(
        local, mesh=mesh, in_specs=placed, out_specs=P("dp", "tensor"), check_vma=False
    )
```
